32 devices in a mesh: lat: 8 (over z, x), tok: 4 (over y, core).
Axes of the slice: x: 2, y: 2, z: 4, core: 2. Of those that a mesh axis runs over, the one named last changes fastest.
Arguments:
- streams: bfloat16 [512, 2, 5120], P('tok', None, 'lat')
- active_mask: int32 [512, 16384], P('tok', 'lat'), may hold values from 0 to 1, as said below
- enc_weight: bfloat16 [16384, 2, 5120], P('lat'), may hold values from -0.0625 to 0.0625
- enc_bias: float32 [16384], P('lat'), may hold values from -3 to 3
- dec_weight: bfloat16 [16384, 2, 5120], P('lat'), may hold values from -0.5 to 0.5
- dec_bias: float32 [2, 5120], replicated, may hold values from -3 to 3
Outputs:
- enc_grad: bfloat16 [16384, 2, 5120], P(('lat', 'tok'))
- dec_grad: bfloat16 [16384, 2, 5120], P(('lat', 'tok'))
- mean_error: float32 [], replicated
The draws below stay inside these ranges and needn't reach their ends.
Inputs may be any that keep to these rules, and one draw needn't show every extreme that they name: `active_mask`: each token has exactly 128 active latents.
All inputs are finite; a program needn't handle non-finite values.
Results may differ from the reference program's by a relative error of at most 0.0065.
Values may be sent and summed in bfloat16 or wider, within the bound.
No kernel may reach another device: no remote copies, remote signals or barrier semaphores. Data moves between devices by JAX's collectives and lax.ppermute only.
A program may use at most 576 MiB of HBM per device.

```python
import math
import jax
import jax.numpy as jnp
from jax import lax

D = 5120
L = 2
H = 16384
TOPK = 128
TOKENS = 512


def draw_streams(key, part):
    subkeys = jax.random.split(key, 3)
    token_pos = jnp.arange(TOKENS, dtype=jnp.float32) / TOKENS
    feature_pos = jnp.arange(D, dtype=jnp.float32) / D
    row_scale = jnp.exp(math.log(3.0) * token_pos + math.log(4.0) * jax.random.uniform(subkeys[0], (TOKENS,), dtype=jnp.float32))
    col_scale = jnp.exp(math.log(3.0) * feature_pos[None, :] + math.log(4.0) * jax.random.uniform(subkeys[1], (L, D), dtype=jnp.float32))
    raw_values = jnp.clip(jax.random.normal(subkeys[2], (TOKENS, L, D), dtype=jnp.float32), -4.0, 4.0)
    return (raw_values * row_scale[:, None, None] * col_scale[None]).astype(jnp.bfloat16)


def draw_active_mask(key, part):
    scores = jax.random.randint(key, (TOKENS, H), 0, 2 ** 31 // H, dtype=jnp.int32)
    scores = scores * H + jnp.arange(H, dtype=jnp.int32)[None, :]
    ranking = jnp.argsort(scores, axis=1, stable=True)
    places = jnp.argsort(ranking, axis=1, stable=True)
    return (places < TOPK).astype(jnp.int32)


def block_levels(own_key, dims, shards, low, largest):
    def one(dim, parts):
        heights = jax.random.uniform(jax.random.fold_in(jax.random.fold_in(own_key, 6), dim), (parts,), jnp.float32, low / len(shards), largest / len(shards))
        return jnp.repeat(jnp.exp(heights), dims[dim] // parts).reshape((-1,) + (1,) * (len(dims) - dim - 1))

    factor_of = one(*shards[0])
    for cut in shards[1:]:
        factor_of = factor_of * one(*cut)
    return factor_of


def gaussian(rng, extent, width, most, cuts=(), held_as=jnp.bfloat16):
    values = jax.random.normal(rng, extent, jnp.float32) * width
    if len(cuts) > 0:
        values = block_levels(rng, extent, cuts, -0.22, 0.18) * values
    return jnp.clip(values, min=-most, max=most).astype(held_as)


def setup_inputs(seed: int = 0) -> dict:
    splits = jax.random.split(jax.random.key(seed), 7)
    return {
        "streams": draw_streams(jax.random.fold_in(splits[6], 71), 0),
        "active_mask": draw_active_mask(jax.random.fold_in(splits[6], 71), 0),
        "enc_weight": gaussian(splits[2], (H, L, D), (L * D) ** -0.5, 0.0625, ((0, 8),)),
        "enc_bias": gaussian(splits[3], (H,), 0.5, 3.0, ((0, 8),), jnp.float32),
        "dec_weight": gaussian(splits[4], (H, L, D), TOPK ** -0.5, 0.5, ((0, 8),)),
        "dec_bias": gaussian(splits[5], (L, D), 0.5, 3.0, (), jnp.float32),
    }


LOSS_SCALE = 128.0

def reference(streams, active_mask, enc_weight, enc_bias, dec_weight, dec_bias):
    stream_f = streams.astype(jnp.float32)
    square_sums = lax.optimization_barrier(jnp.sum(stream_f * stream_f, axis=(0, 2)))
    norm_scale = lax.rsqrt(square_sums / (TOKENS * D) + 1e-06)
    enc_parts = jnp.einsum('tld,hld->lth', stream_f, enc_weight.astype(jnp.float32))
    pre_act = lax.optimization_barrier(jnp.sum(norm_scale[:, None, None] * enc_parts, axis=0)) + enc_bias[None, :]
    mask_float = active_mask.astype(jnp.float32)
    act_low = (mask_float * pre_act).astype(jnp.bfloat16)
    dec_flat = dec_weight.reshape(H, L * D)
    recon = jnp.dot(act_low, dec_flat, preferred_element_type=jnp.float32).reshape(TOKENS, L, D) + dec_bias[None]
    diff = recon - norm_scale[None, :, None] * stream_f
    mean_error = jnp.sum(diff * diff) / (TOKENS * L * D)
    err_low = (diff * (LOSS_SCALE / TOKENS)).astype(jnp.bfloat16)
    err_flat = err_low.reshape(TOKENS, L * D)
    lat_grad = jnp.dot(err_flat, dec_flat.T, preferred_element_type=jnp.float32)
    grad_low = (mask_float * lat_grad).astype(jnp.bfloat16)
    dec_grad = jnp.dot(act_low.T, err_flat, preferred_element_type=jnp.float32).reshape(H, L, D)
    enc_sum = jnp.dot(grad_low.T, streams.reshape(TOKENS, L * D), preferred_element_type=jnp.float32).reshape(H, L, D)
    enc_grad = enc_sum * norm_scale[None, :, None]
    return (enc_grad.astype(jnp.bfloat16), dec_grad.astype(jnp.bfloat16), mean_error)
```

```python
import functools

import jax
import jax.numpy as jnp
from jax import lax
from jax.experimental import pallas as pl
from jax.experimental.pallas import tpu as pltpu
from jax.sharding import PartitionSpec as P

LOSS_SCALE = 128.0
LANES = 128
BF16 = jnp.bfloat16
F32 = jnp.float32
LATENT_ROWS = 256
VMEM_BYTES = 63 * 1024 * 1024
SMALL = pl.CostEstimate(flops=1024, bytes_accessed=1024, transcendentals=0)


def exchange(value, axis, mask):
    size = lax.axis_size(axis)
    return lax.ppermute(value, axis, [(i, i ^ mask) for i in range(size)])


def after(value, *others):
    return lax.optimization_barrier((value, *others))[0]


def sum_tokens(value):
    step = 1
    while step < lax.axis_size("tok"):
        value = value + exchange(value, "tok", step)
        step *= 2
    return value


def squares_kernel(ref, out_ref):
    layers, sub, lanes = out_ref.shape
    count, height, width = ref.shape
    tokens = height // layers
    for l in range(layers):
        sums = []
        for i in range(count):
            value = ref[i, l * tokens:(l + 1) * tokens, :].astype(F32)
            value = jnp.sum((value * value).reshape(tokens // sub, sub, width), axis=0)
            total = value[:, :lanes]
            for c in range(1, width // lanes):
                total = total + value[:, c * lanes:(c + 1) * lanes]
            sums.append(total)
        while len(sums) > 1:
            sums = [sums[i] + sums[i + 1] for i in range(0, len(sums), 2)]
        out_ref[l] = sums[0]


def squares(stacked, layers):
    return pl.pallas_call(
        squares_kernel,
        out_shape=jax.ShapeDtypeStruct((layers, 8, LANES), F32),
        compiler_params=pltpu.CompilerParams(vmem_limit_bytes=VMEM_BYTES),
        cost_estimate=SMALL,
        name="squares",
    )(stacked)


def block_order(count):
    return list(range(0, count, 2)), list(range(1, count, 2))


def gather_features(own, beside=(), over_tok=False):
    beside = list(beside)
    count = lax.axis_size("lat")
    if own.shape[1] % LANES:
        blocks = jnp.split(lax.all_gather(own, "lat", axis=1, tiled=True), 8, axis=1)
        return blocks, {k: exchange(block, "tok", 2) for k, block in enumerate(blocks) if over_tok}
    direct = {}
    step = count // 2
    while step:
        direct[step] = exchange(own, "lat", step)
        step //= 2
    held = {0: own}
    crossed = {1: direct[1]}
    far = {k: exchange(value, "tok", 2) for k, value in ((0, own), (1, direct[1])) if over_tok}
    early = [value for k, value in direct.items() if k < count // 2]
    early += [far[k] for k in far if k == 0]
    step = count // 2
    while step > 1:
        if beside:
            early += beside.pop(0)
        fresh = {
            k | step: exchange(value, "lat", step) if k else direct[step] for k, value in held.items()
        }
        for k, value in held.items():
            if k | 1 not in crossed:
                crossed[k | 1] = exchange(value, "lat", 1)
                early.append(crossed[k | 1])
        if step < count // 2:
            if over_tok:
                for k in (count // 2, step):
                    far[k] = exchange(held.get(k, direct[k]), "tok", 2)
                    early.append(far[k])
                early.append(far[1])
            else:
                crossed[step | 1] = exchange(direct[step], "lat", 1)
                early.append(crossed[step | 1])
        for k, value in fresh.items():
            held[k] = value if k in direct and k < count // 2 else after(value, *early)
        early = []
        step //= 2
    for k, value in held.items():
        if k | 1 not in crossed:
            crossed[k | 1] = exchange(value, "lat", 1)
    held.update(crossed)
    if over_tok:
        far.update({k: exchange(held[k], "tok", 2) for k in held if k not in far})
    return [held[k] for k in range(count)], far


def stack_kernel(*refs):
    for i, ref in enumerate(refs[:-1]):
        refs[-1][i] = ref[...]


def stack(blocks):
    return pl.pallas_call(
        stack_kernel,
        out_shape=jax.ShapeDtypeStruct((len(blocks), *blocks[0].shape), blocks[0].dtype),
        compiler_params=pltpu.CompilerParams(vmem_limit_bytes=VMEM_BYTES),
        cost_estimate=SMALL,
        name="stack",
    )(*blocks)


def scatter_features(pieces):
    pieces = dict(pieces)
    step = 4
    while step < lax.axis_size("lat"):
        for k in sorted(pieces, reverse=True):
            if k & step:
                sent = pieces.pop(k).astype(BF16)
                pieces[k ^ step] = pieces[k ^ step] + exchange(sent, "lat", step).astype(F32)
        step *= 2
    return pieces[0]


def run_slices(value, mask, axis):
    count = lax.axis_size("tok")
    rows = value.shape[axis] // count
    me = lax.axis_index("tok") ^ mask
    return jnp.concatenate(
        [lax.dynamic_slice_in_dim(value, (me ^ r) * rows, rows, axis) for r in range(0, count, 2)],
        axis=axis,
    )


def weight_copies(place, w_ref, buffer, sems, half):
    latents, layers, full = w_ref.shape
    pairs, parts, height, width = buffer.shape
    block = width // 2
    runs = lax.axis_size("tok") // 2
    quarter = layers * latents // (2 * runs)
    rows = min(height, quarter)
    pieces = height // rows
    flat = w_ref.reshape(latents * layers, full)

    def copies_of(pair, part):
        copies = []
        for piece in range(pieces):
            run, row = divmod(part * height + piece * rows, quarter)
            start = (place[1] ^ (2 * run)) * quarter + row
            for b in range(2):
                column = (place[0] ^ half[2 * pair + b]) * block
                copies.append(
                    pltpu.make_async_copy(
                        flat.at[
                            pl.ds(pl.multiple_of(start, rows), rows),
                            pl.ds(pl.multiple_of(column, LANES), block),
                        ],
                        buffer.at[pair, part, pl.ds(piece * rows, rows), pl.ds(b * block, block)],
                        sems.at[((pair * parts + part) * pieces + piece) * 2 + b],
                    )
                )
        return copies

    return copies_of


def weight_buffers(weight, half, block):
    latents, layers, full = weight.shape
    runs = lax.axis_size("tok") // 2
    quarter = latents // (2 * runs)
    rows = min(LATENT_ROWS, runs * quarter)
    parts = runs * quarter // rows
    pieces = max(1, rows // quarter)
    pairs = len(half) // 2
    return (
        pltpu.VMEM((pairs, parts, layers * rows, 2 * block), BF16),
        pltpu.SemaphoreType.DMA((pairs * parts * pieces * 2,)),
    )


def encode_kernel(place, w_ref, *refs, half, mode, earlier):
    blocks = refs[:2]
    sums = refs[2:2 + earlier]
    buffer, sems, values, scratch = refs[-4:]
    rest = refs[2 + earlier:-4]
    layers = w_ref.shape[1]
    count, height, width = blocks[0].shape
    tokens = height // layers
    pairs, parts, rows, _ = buffer.shape
    step = pl.program_id(0)
    copies_of = weight_copies(place, w_ref, buffer, sems, half)

    @pl.when(step == 0)
    def _():
        for part in range(parts):
            for pair in range(pairs):
                for copy in copies_of(pair, part):
                    copy.start()
        for l in range(layers):
            for e, ref in enumerate(blocks):
                start = (2 * l + e) * tokens
                for i in range(count):
                    values[start:start + tokens, i * width:(i + 1) * width] = ref[
                        i, l * tokens:(l + 1) * tokens, :
                    ]

    for part in range(parts):

        @pl.when(step == part)
        def _():
            for pair in range(pairs):
                for copy in copies_of(pair, part):
                    copy.wait()

    product = None
    for pair in range(pairs):
        term = lax.dot_general(
            buffer[pair, step],
            values[:, pair * 2 * width:(pair + 1) * 2 * width],
            (((1,), (1,)), ((), ())),
            preferred_element_type=F32,
        )
        product = term if product is None else product + term
    sums_of = []
    for l in range(layers):
        for e in range(2):
            scratch[l, e] = product[:, (2 * l + e) * tokens:(2 * l + e + 1) * tokens]
        sums_of.append(
            jnp.concatenate(
                [scratch[l, e, pl.ds(l, rows // layers, stride=layers)] for e in range(2)], axis=1
            )
        )
    if mode == "parts":
        for l in range(layers):
            rest[0][l] = sums_of[l]
    else:
        norm_ref, bias_ref, mask_ref, across_ref, act_ref = rest
        for ref in sums:
            sums_of = [value + ref[l] for l, value in enumerate(sums_of)]
        pre = norm_ref[0] * sums_of[0] + norm_ref[1] * sums_of[1] + bias_ref[...]
        act = mask_ref[...].astype(F32).T * pre
        act_ref[...] = act.astype(BF16)
        across_ref[...] = act.T.astype(BF16)


def encode(weight, half, own, near, place, mode, sums=(), norm=None, bias=None, mask=None):
    layers, full = weight.shape[1:]
    tokens = 2 * own.shape[1] // layers
    block = own.shape[2]
    buffer, sems = weight_buffers(weight, half, block)
    _, parts, height, _ = buffer.shape
    rows = height // layers
    latents = parts * rows
    whole = pl.BlockSpec(own.shape, lambda i, s: (0, 0, 0))
    flat = pl.BlockSpec((rows, tokens), lambda i, s: (i, 0))
    split = pl.BlockSpec((layers, rows, tokens), lambda i, s: (0, i, 0))
    in_specs = [pl.BlockSpec(memory_space=pl.ANY)] + [whole] * 2
    in_specs += [flat if value.ndim == 2 else split for value in sums]
    args = [weight, own, near, *sums]
    if mode == "act":
        across = pl.BlockSpec((tokens, rows), lambda i, s: (0, i))
        in_specs += [
            pl.BlockSpec(memory_space=pltpu.SMEM),
            pl.BlockSpec((rows, 1), lambda i, s: (i, 0)),
            across,
        ]
        args += [norm, bias, mask]
        out_specs = (across, flat)
        out_shape = (
            jax.ShapeDtypeStruct((tokens, latents), BF16),
            jax.ShapeDtypeStruct((latents, tokens), BF16),
        )
    else:
        out_specs = split
        out_shape = jax.ShapeDtypeStruct((layers, latents, tokens), F32)
    return pl.pallas_call(
        functools.partial(encode_kernel, half=half, mode=mode, earlier=len(sums)),
        grid_spec=pltpu.PrefetchScalarGridSpec(
            num_scalar_prefetch=1,
            grid=(parts,),
            in_specs=in_specs,
            out_specs=out_specs,
            scratch_shapes=[
                buffer,
                sems,
                pltpu.VMEM((layers * tokens, len(half) * block), BF16),
                pltpu.VMEM((layers, 2, height, tokens // 2), F32),
            ],
        ),
        out_shape=out_shape,
        compiler_params=pltpu.CompilerParams(vmem_limit_bytes=VMEM_BYTES),
        cost_estimate=SMALL,
        name="encode_" + mode,
    )(place, *args)


def rearrange_kernel(place, *refs, halves, count):
    parts = refs[:count]
    outs = refs[-3:-1]
    wide = refs[-1]
    rows, layers, full = parts[0].shape
    chunks = full // LANES
    each = outs[0].shape[2] // len(halves[0]) // LANES
    for p, w_ref in enumerate(parts):
        for c in range(chunks):
            wide[c] = (
                w_ref[:, :, c * LANES:(c + 1) * LANES].reshape(rows * layers, LANES).astype(F32)
            )
        for half, out_ref in zip(halves, outs):
            for i, k in enumerate(half):
                for c in range(each):
                    chunk = (place[0] ^ k) * each + c
                    column = (i * each + c) * LANES
                    for l in range(layers):
                        out_ref[l, p * rows:(p + 1) * rows, column:column + LANES] = wide[
                            chunk, pl.ds(l, rows, stride=layers)
                        ].astype(BF16)


def rearrange(weight, place, halves, runs, run, earlier=()):
    latents, layers, full = weight.shape
    quarter = latents // (2 * runs)
    part = min(64, quarter // 2)
    count = 2
    rows = count * part
    steps = quarter // rows

    def index_of(p):
        return lambda i, s: (((s[1] ^ (2 * run)) * steps + i) * count + p, 0, 0)

    out = pl.BlockSpec((layers, rows, full // 2), lambda i, s: (0, run * steps + i, 0))
    shape = jax.ShapeDtypeStruct((layers, runs * quarter, full // 2), BF16)
    return pl.pallas_call(
        functools.partial(rearrange_kernel, halves=halves, count=count),
        grid_spec=pltpu.PrefetchScalarGridSpec(
            num_scalar_prefetch=1,
            grid=(steps,),
            in_specs=[pl.BlockSpec((part, layers, full), index_of(p)) for p in range(count)]
            + [pl.BlockSpec(memory_space=pl.ANY)] * len(earlier),
            out_specs=(out, out),
            scratch_shapes=[pltpu.VMEM((full // LANES, part * layers, LANES), F32)],
        ),
        out_shape=(shape, shape),
        input_output_aliases={1 + count + i: i for i in range(len(earlier))},
        compiler_params=pltpu.CompilerParams(vmem_limit_bytes=VMEM_BYTES),
        cost_estimate=SMALL,
        name="rearrange",
    )(place, *[weight] * count, *earlier)


def project_kernel(*refs, layers, mode, earlier):
    w_refs = refs[:layers]
    blocks = refs[layers:layers + 2]
    sums = refs[layers + 2:layers + 2 + earlier]
    values = refs[-1]
    rest = refs[layers + 2 + earlier:-1]
    count, height, width = blocks[0].shape
    tokens = height // layers

    @pl.when(pl.program_id(0) == 0)
    def _():
        for e, ref in enumerate(blocks):
            for l in range(layers):
                for i in range(count):
                    values[l, e * tokens:(e + 1) * tokens, i * width:(i + 1) * width] = ref[
                        i, l * tokens:(l + 1) * tokens, :
                    ]

    parts = [
        lax.dot_general(
            w_refs[l][0], values[l], (((1,), (1,)), ((), ())), preferred_element_type=F32
        )
        for l in range(layers)
    ]
    if mode == "sum":
        rest[0][...] = parts[0] + parts[1]
    else:
        mask_ref, grad_ref = rest
        total = parts[0] + parts[1]
        for ref in sums:
            total = total + ref[...]
        grad_ref[...] = (mask_ref[...].astype(F32).T * total).astype(BF16)


def project(matrix, own, near, mode, sums=(), mask=None):
    layers, latents, width = matrix.shape
    tokens = 2 * own.shape[1] // layers
    rows = min(LATENT_ROWS, latents)
    whole = pl.BlockSpec(own.shape, lambda i: (0, 0, 0))
    flat = pl.BlockSpec((rows, tokens), lambda i: (i, 0))
    across = pl.BlockSpec((tokens, rows), lambda i: (0, i))

    def layer(l):
        return pl.BlockSpec((1, rows, width), lambda i: (l, i, 0))

    in_specs = [layer(l) for l in range(layers)] + [whole] * 2
    in_specs += [flat] * len(sums)
    args = [matrix] * layers + [own, near, *sums]
    if mode == "grad":
        in_specs.append(across)
        args.append(mask)
    out_specs = flat
    out_shape = jax.ShapeDtypeStruct((latents, tokens), BF16 if mode == "grad" else F32)
    return pl.pallas_call(
        functools.partial(project_kernel, layers=layers, mode=mode, earlier=len(sums)),
        grid=(latents // rows,),
        in_specs=in_specs,
        out_specs=out_specs,
        scratch_shapes=[pltpu.VMEM((layers, tokens, width), BF16)],
        out_shape=out_shape,
        compiler_params=pltpu.CompilerParams(vmem_limit_bytes=VMEM_BYTES),
        cost_estimate=SMALL,
        name="project_" + mode,
    )(*args)


def recon_kernel(act_ref, *refs, parts):
    w_refs = refs[:parts]
    keep_ref = refs[parts]
    send_refs = refs[parts + 1:]
    depth = w_refs[0].shape[1]
    product = None
    for p, w_ref in enumerate(w_refs):
        term = jnp.dot(
            act_ref[:, p * depth:(p + 1) * depth], w_ref[0], preferred_element_type=F32
        )
        product = term if product is None else product + term
    blocks, own, width = keep_ref.shape
    for i in range(blocks):
        keep_ref[i] = product[:own, i * width:(i + 1) * width]
    if len(send_refs) == 1:
        for i in range(blocks):
            send_refs[0][i] = product[own:, i * width:(i + 1) * width].astype(BF16)
    else:
        for pair in range(len(send_refs) // 2):

            @pl.when(pl.program_id(0) == pair)
            def _():
                for i in range(2):
                    send_refs[2 * pair + i][...] = product[
                        own:, i * width:(i + 1) * width
                    ].astype(BF16)


def recon_half(act, matrix, blocks, apart):
    layers, latents, full = matrix.shape
    width = full // blocks
    tokens = act.shape[0] // 2
    parts = 2

    def part(p):
        return pl.BlockSpec((1, latents // parts, 2 * width), lambda i, j: (j, p, i))

    def single(b):
        def index(i, j):
            return jnp.where(i < b // 2, 0, jnp.where(i > b // 2, layers - 1, j)), 0

        return pl.BlockSpec((tokens, width), index)

    out = pl.BlockSpec((2, tokens, width), lambda i, j: (i, j, 0))
    shape = (blocks, layers * tokens, width)
    if apart:
        send_specs = [single(b) for b in range(blocks)]
        send_shapes = [jax.ShapeDtypeStruct(shape[1:], BF16)] * blocks
    else:
        send_specs, send_shapes = [out], [jax.ShapeDtypeStruct(shape, BF16)]
    keep, *send = pl.pallas_call(
        functools.partial(recon_kernel, parts=parts),
        grid=(blocks // 2, layers),
        in_specs=[pl.BlockSpec(act.shape, lambda i, j: (0, 0))] + [part(p) for p in range(parts)],
        out_specs=[out] + send_specs,
        out_shape=[jax.ShapeDtypeStruct(shape, F32)] + send_shapes,
        compiler_params=pltpu.CompilerParams(vmem_limit_bytes=VMEM_BYTES),
        cost_estimate=SMALL,
        name="recon_half",
    )(act, *[matrix] * parts)
    return keep, send


def grad_kernel(place, scale_ref, own_ref, far_ref, *refs, groups, where, sources, scaled):
    value_refs = refs[:sources]
    out_ref, values, left, wide, results, sems, out_sems = refs[sources:]
    pair, pairs = pl.program_id(0), pl.num_programs(0)
    pairs_held, layers, depth, width = values.shape
    tokens = depth // groups
    half = width // 2
    rows = out_ref.shape[0]
    blocks = len(where) // groups
    flat = out_ref.reshape(rows * layers, out_ref.shape[2])

    def copy_of(g, k, l):
        side = (k % 2) ^ place[1]
        source, index = where[g * blocks + k]
        if source is None:
            piece = value_refs[index[0]].at[place[2] ^ g, index[1]]
        elif index < 0:
            piece = value_refs[source]
        else:
            piece = value_refs[source].at[index]
        return pltpu.make_async_copy(
            piece.at[pl.ds(l * tokens, tokens)],
            values.at[
                k // 2, l, pl.ds(g * tokens, tokens), pl.ds(pl.multiple_of(side * half, LANES), half)
            ],
            sems.at[(g * blocks + k) * layers + l],
        )

    def copy_out(turn):
        return pltpu.make_async_copy(
            results.at[lax.rem(turn, 2)],
            flat.at[:, pl.ds(pl.multiple_of((place[0] ^ turn) * width, LANES), width)],
            out_sems.at[lax.rem(turn, 2)],
        )

    @pl.when(pair == 0)
    def _():
        for k in range(blocks):
            for g in range(groups):
                for l in range(layers):
                    copy_of(g, k, l).start()
        near = own_ref.shape[1]
        left[:, :near] = own_ref[...]
        left[:, near:] = far_ref[...]

    for j in range(blocks // 2):

        @pl.when(pair == j)
        def _():
            for b in range(2):
                for g in range(groups):
                    for l in range(layers):
                        copy_of(g, 2 * j + b, l).wait()

    for l in range(layers):
        product = jnp.dot(left[...], values[pair, l], preferred_element_type=F32)
        if scaled:
            product = product * scale_ref[l]
        for c in range(width // LANES):
            wide[c, pl.ds(l, rows, stride=layers)] = product[:, c * LANES:(c + 1) * LANES]

    @pl.when(pair >= 2)
    def _():
        copy_out(pair - 2).wait()

    for c in range(width // LANES):
        results[lax.rem(pair, 2), :, c * LANES:(c + 1) * LANES] = wide[c].astype(BF16)
    copy_out(pair).start()

    @pl.when(pair == pairs - 1)
    def _():
        copy_out(pair - 1).wait()
        copy_out(pair).wait()


def weight_grad(own, far, sources, where, place, scale, scaled, shape):
    rows = far.shape[0]
    layers, full = shape
    groups = lax.axis_size("tok")
    depth = own.shape[1] + far.shape[1]
    blocks = len(where) // groups
    width = full // (blocks // 2)
    anywhere = pl.BlockSpec(memory_space=pl.ANY)
    return pl.pallas_call(
        functools.partial(
            grad_kernel, groups=groups, where=where, sources=len(sources), scaled=scaled
        ),
        grid_spec=pltpu.PrefetchScalarGridSpec(
            num_scalar_prefetch=1,
            grid=(blocks // 2,),
            in_specs=[
                pl.BlockSpec(memory_space=pltpu.SMEM),
                pl.BlockSpec(far.shape, lambda i, s: (0, 0)),
                pl.BlockSpec(far.shape, lambda i, s: (0, 0)),
            ]
            + [anywhere] * len(sources),
            out_specs=anywhere,
            scratch_shapes=[
                pltpu.VMEM((blocks // 2, layers, depth, width), BF16),
                pltpu.VMEM((rows, depth), BF16),
                pltpu.VMEM((width // LANES, rows * layers, LANES), F32),
                pltpu.VMEM((2, rows * layers, width), BF16),
                pltpu.SemaphoreType.DMA((groups * blocks * layers,)),
                pltpu.SemaphoreType.DMA((2,)),
            ],
        ),
        out_shape=jax.ShapeDtypeStruct((rows, layers, full), BF16),
        compiler_params=pltpu.CompilerParams(vmem_limit_bytes=VMEM_BYTES),
        cost_estimate=SMALL,
        name="weight_grad",
    )(place, scale, own, far, *sources)


def per_device(streams, active_mask, enc_weight, enc_bias, dec_weight, dec_bias):
    lat_count = lax.axis_size("lat")
    tok_count = lax.axis_size("tok")
    tok_dev, layers, width_part = streams.shape
    full_width = width_part * lat_count
    tokens = tok_dev * tok_count
    me = lax.axis_index("lat")
    aligned = width_part % LANES == 0
    block_count = lat_count if aligned else 8
    block_width = full_width // block_count
    here = me if aligned else jnp.zeros_like(me)

    own_x = streams.transpose(1, 0, 2).reshape(layers * tok_dev, width_part)
    own_f = own_x.astype(F32).reshape(layers, tok_dev, width_part)
    runs = tok_count // 2
    tok_me = lax.axis_index("tok")
    halves = block_order(block_count)
    spot = jnp.stack([here, tok_me]).astype(jnp.int32)
    place = jnp.stack([here >> 1, here & 1, tok_me]).astype(jnp.int32)

    mask_low = active_mask.astype(BF16)
    mask_far = exchange(run_slices(mask_low, 1, 1), "tok", 1)
    mask = jnp.concatenate([run_slices(mask_low, 0, 1), mask_far], axis=0)
    bias = run_slices(enc_bias.reshape(-1, 1), 0, 0)

    def gather_halves(own, multiply, beside=(), over_tok=False):
        blocks, far = gather_features(own, beside, over_tok)
        first = stack([blocks[k] for k in halves[0]])
        first_near = exchange(first, "tok", 1)
        sums = multiply(first, first_near)
        squared = squares(first, layers)
        early = [sums, squared]
        if over_tok:
            early += [far[k] for k in (6, 5)]
        final = halves[1][-1]
        blocks[final] = after(blocks[final], *early)
        second = stack([blocks[k] for k in halves[1]])
        near = [first_near, exchange(second, "tok", 1)]
        return [first, second], near, sums, squared, far

    dec_first = rearrange(dec_weight, spot, halves, runs, 0)
    dec_halves = rearrange(dec_weight, spot, halves, runs, 1, dec_first)
    x_own, x_near, sums, squared, _ = gather_halves(
        own_x,
        lambda own, near: encode(enc_weight, halves[0], own, near, spot, "parts"),
        beside=([*dec_first, mask, bias], dec_halves),
    )
    square_sums = jnp.sum(sum_tokens(squared + squares(x_own[1], layers)), axis=(1, 2))
    norm_scale = lax.rsqrt(square_sums / (tokens * full_width) + 1e-06)
    act_across, act = encode(
        enc_weight, halves[1], x_own[1], x_near[1], spot, "act", [sums], norm_scale, bias, mask
    )
    x_all = [lax.all_gather(value, "tok") for value in x_own]
    quarter = act.shape[0] // runs

    bias_part = lax.dynamic_slice_in_dim(dec_bias, me * width_part, width_part, 1)
    keep, send = recon_half(act_across, dec_halves[1], block_count // 2, False)
    cross = keep + exchange(send[0], "tok", 1).astype(F32)
    starts = range(block_count // 2 - 2, -2, -2)
    if aligned:
        bundles = [cross[start:start + 2].astype(BF16) for start in starts]
        act_across = after(act_across, *bundles)
        bundles = [exchange(bundle, "lat", 1) for bundle in bundles]
    keep, send = recon_half(act_across, dec_halves[0], block_count // 2, True)
    send = [exchange(value, "tok", 1) for value in send]
    act_far = exchange(act[quarter:], "tok", 2)
    if aligned:
        pieces = {}
        received = None
        for start, bundle in zip(starts, bundles):
            if received is not None:
                bundle = after(bundle, received)
            low, high = [
                keep[i] + send[i].astype(F32) + bundle[i - start].astype(F32)
                for i in (start, start + 1)
            ]
            received = exchange(high.astype(BF16), "lat", 2)
            pieces[2 * start] = low + received.astype(F32)
        recon = scatter_features(pieces)
    else:
        own = keep + jnp.stack(send).astype(F32)
        whole = jnp.stack([own, cross], axis=1).reshape(block_count, layers * tok_dev, block_width)
        whole = whole.transpose(1, 0, 2).reshape(layers * tok_dev, full_width)
        recon = lax.psum_scatter(whole, "lat", scatter_dimension=1, tiled=True)
    recon = after(recon, act_far, *x_all)

    recon = recon.reshape(layers, tok_dev, width_part) + bias_part[:, None]
    diff = recon - norm_scale[:, None, None] * own_f
    factor = LOSS_SCALE / tokens
    err_low = (diff * factor).astype(BF16).reshape(layers * tok_dev, width_part)
    err_own, err_near, sums, squared, far = gather_halves(
        err_low, lambda own, near: project(dec_halves[0], own, near, "sum"), over_tok=True
    )
    grad = project(dec_halves[1], err_own[1], err_near[1], "grad", [sums], mask=mask)
    grad_far = exchange(grad[quarter:], "tok", 2)
    error_sums = squared + squares(err_own[1], layers)
    soon = [k for k in range(block_count) if k not in (3, 7)]
    last = {k: exchange(far[k], "tok", 1) for k in soon}
    grad_far, error_sums, far[3], far[7] = lax.optimization_barrier(
        (grad_far, error_sums, far[3], far[7])
    )

    shape = (layers, full_width)
    spots = {k: (h, i) for h, half in enumerate(halves) for i, k in enumerate(half)}
    order = [spots[k] for k in range(block_count)]
    enc_grad = weight_grad(
        grad, grad_far, x_all, [(None, spot) for spot in order] * tok_count, place,
        norm_scale, True, shape,
    )
    error_sums = error_sums + exchange(error_sums, "tok", 1)
    act, error_sums = lax.optimization_barrier((act, error_sums))
    for k in (3, 7):
        last[k] = exchange(far[k], "tok", 1)
    where = [(2 * g + h, i) for g in range(2) for h, i in order]
    where += [(4 + g * block_count + k, -1) for g in range(2) for k in range(block_count)]
    sources = err_own + err_near + [group[k] for group in (far, last) for k in range(block_count)]
    dec_grad = weight_grad(act, act_far, sources, where, place, norm_scale, False, shape)
    error_sum = jnp.sum(error_sums + exchange(error_sums, "tok", 2))
    mean_error = error_sum / (factor * factor * tokens * layers * full_width)
    return (enc_grad, dec_grad, mean_error)


def solution(mesh):
    in_specs = (
        P("tok", None, "lat"),
        P("tok", "lat"),
        P("lat", None, None),
        P("lat"),
        P("lat", None, None),
        P(),
    )
    out_specs = (P(("lat", "tok"), None, None), P(("lat", "tok"), None, None), P())
    return jax.shard_map(
        per_device, mesh=mesh, in_specs=in_specs, out_specs=out_specs, check_vma=False
    )
```

```python
import functools

import jax
import jax.numpy as jnp
from jax import lax
from jax.experimental import pallas as pl
from jax.experimental.pallas import tpu as pltpu
from jax.sharding import PartitionSpec as P

LOSS_SCALE = 128.0
LANES = 128
BF16 = jnp.bfloat16
F32 = jnp.float32
LATENT_ROWS = 256
VMEM_BYTES = 63 * 1024 * 1024
SMALL = pl.CostEstimate(flops=1024, bytes_accessed=1024, transcendentals=0)


def exchange(value, axis, mask):
    size = lax.axis_size(axis)
    return lax.ppermute(value, axis, [(i, i ^ mask) for i in range(size)])


def after(value, *others):
    return lax.optimization_barrier((value, *others))[0]


def sums_over(value, axis):
    sums = []
    step = lax.axis_size(axis) // 2
    while step:
        value = value + exchange(value, axis, step)
        sums.append(value)
        step //= 2
    return sums


def squares_kernel(ref, out_ref):
    layers, sub, lanes = out_ref.shape
    count, height, width = ref.shape
    tokens = height // layers
    for l in range(layers):
        sums = []
        for i in range(count):
            value = ref[i, l * tokens:(l + 1) * tokens, :].astype(F32)
            value = jnp.sum((value * value).reshape(tokens // sub, sub, width), axis=0)
            total = value[:, :lanes]
            for c in range(1, width // lanes):
                total = total + value[:, c * lanes:(c + 1) * lanes]
            sums.append(total)
        while len(sums) > 1:
            sums = [sums[i] + sums[i + 1] for i in range(0, len(sums), 2)]
        out_ref[l] = sums[0]


def squares(stacked, layers):
    return pl.pallas_call(
        squares_kernel,
        out_shape=jax.ShapeDtypeStruct((layers, 8, LANES), F32),
        compiler_params=pltpu.CompilerParams(vmem_limit_bytes=VMEM_BYTES),
        cost_estimate=SMALL,
        name="squares",
    )(stacked)


def block_order(count):
    return list(range(0, count, 2)), list(range(1, count, 2))


def gather_features(own, beside=(), over_tok=False):
    beside = list(beside)
    count = lax.axis_size("lat")
    if own.shape[1] % LANES:
        blocks = jnp.split(lax.all_gather(own, "lat", axis=1, tiled=True), 8, axis=1)
        return blocks, {k: exchange(block, "tok", 2) for k, block in enumerate(blocks) if over_tok}
    direct = {}
    step = count // 2
    while step:
        direct[step] = exchange(own, "lat", step)
        step //= 2
    held = {0: own}
    crossed = {1: direct[1]}
    far = {k: exchange(value, "tok", 2) for k, value in ((0, own), (1, direct[1])) if over_tok}
    early = [value for k, value in direct.items() if k < count // 2]
    early += [far[k] for k in far if k == 0]
    step = count // 2
    while step > 1:
        if beside:
            early += beside.pop(0)
        fresh = {
            k | step: exchange(value, "lat", step) if k else direct[step] for k, value in held.items()
        }
        for k, value in held.items():
            if k | 1 not in crossed:
                crossed[k | 1] = exchange(value, "lat", 1)
                early.append(crossed[k | 1])
        if step < count // 2:
            if over_tok:
                early.append(far[1])
            else:
                crossed[step | 1] = exchange(direct[step], "lat", 1)
                early.append(crossed[step | 1])
        for k, value in fresh.items():
            held[k] = value if k in direct and k < count // 2 else after(value, *early)
        early = []
        step //= 2
    for k, value in held.items():
        if k | 1 not in crossed:
            crossed[k | 1] = exchange(value, "lat", 1)
    held.update(crossed)
    if over_tok:
        far.update({k: exchange(held[k], "tok", 2) for k in held if k not in far})
    return [held[k] for k in range(count)], far


def stack_kernel(*refs):
    for i, ref in enumerate(refs[:-1]):
        refs[-1][i] = ref[...]


def stack(blocks):
    return pl.pallas_call(
        stack_kernel,
        out_shape=jax.ShapeDtypeStruct((len(blocks), *blocks[0].shape), blocks[0].dtype),
        compiler_params=pltpu.CompilerParams(vmem_limit_bytes=VMEM_BYTES),
        cost_estimate=SMALL,
        name="stack",
    )(*blocks)


def scatter_features(pieces):
    pieces = dict(pieces)
    step = 4
    while step < lax.axis_size("lat"):
        for k in sorted(pieces, reverse=True):
            if k & step:
                sent = pieces.pop(k).astype(BF16)
                pieces[k ^ step] = pieces[k ^ step] + exchange(sent, "lat", step).astype(F32)
        step *= 2
    return pieces[0]


def run_slices(value, mask, axis):
    count = lax.axis_size("tok")
    rows = value.shape[axis] // count
    me = lax.axis_index("tok") ^ mask
    return jnp.concatenate(
        [lax.dynamic_slice_in_dim(value, (me ^ r) * rows, rows, axis) for r in range(0, count, 2)],
        axis=axis,
    )


def weight_copies(place, w_ref, buffer, sems, half):
    latents, layers, full = w_ref.shape
    pairs, parts, height, width = buffer.shape
    block = width // 2
    runs = lax.axis_size("tok") // 2
    quarter = layers * latents // (2 * runs)
    rows = min(height, quarter)
    pieces = height // rows
    flat = w_ref.reshape(latents * layers, full)

    def copies_of(pair, part):
        copies = []
        for piece in range(pieces):
            run, row = divmod(part * height + piece * rows, quarter)
            start = (place[1] ^ (2 * run)) * quarter + row
            for b in range(2):
                column = (place[0] ^ half[2 * pair + b]) * block
                copies.append(
                    pltpu.make_async_copy(
                        flat.at[
                            pl.ds(pl.multiple_of(start, rows), rows),
                            pl.ds(pl.multiple_of(column, LANES), block),
                        ],
                        buffer.at[pair, part, pl.ds(piece * rows, rows), pl.ds(b * block, block)],
                        sems.at[((pair * parts + part) * pieces + piece) * 2 + b],
                    )
                )
        return copies

    return copies_of


def weight_buffers(weight, half, block):
    latents, layers, full = weight.shape
    runs = lax.axis_size("tok") // 2
    quarter = latents // (2 * runs)
    rows = min(LATENT_ROWS, runs * quarter)
    parts = runs * quarter // rows
    pieces = max(1, rows // quarter)
    pairs = len(half) // 2
    return (
        pltpu.VMEM((pairs, parts, layers * rows, 2 * block), BF16),
        pltpu.SemaphoreType.DMA((pairs * parts * pieces * 2,)),
    )


def encode_kernel(place, w_ref, *refs, half, mode, earlier):
    blocks = refs[:2]
    sums = refs[2:2 + earlier]
    buffer, sems, values, scratch = refs[-4:]
    rest = refs[2 + earlier:-4]
    layers = w_ref.shape[1]
    count, height, width = blocks[0].shape
    tokens = height // layers
    pairs, parts, rows, _ = buffer.shape
    step = pl.program_id(0)
    copies_of = weight_copies(place, w_ref, buffer, sems, half)

    @pl.when(step == 0)
    def _():
        for part in range(parts):
            for pair in range(pairs):
                for copy in copies_of(pair, part):
                    copy.start()
        for l in range(layers):
            for e, ref in enumerate(blocks):
                start = (2 * l + e) * tokens
                for i in range(count):
                    values[start:start + tokens, i * width:(i + 1) * width] = ref[
                        i, l * tokens:(l + 1) * tokens, :
                    ]

    for part in range(parts):

        @pl.when(step == part)
        def _():
            for pair in range(pairs):
                for copy in copies_of(pair, part):
                    copy.wait()

    product = None
    for pair in range(pairs):
        term = lax.dot_general(
            buffer[pair, step],
            values[:, pair * 2 * width:(pair + 1) * 2 * width],
            (((1,), (1,)), ((), ())),
            preferred_element_type=F32,
        )
        product = term if product is None else product + term
    sums_of = []
    for l in range(layers):
        for e in range(2):
            scratch[l, e] = product[:, (2 * l + e) * tokens:(2 * l + e + 1) * tokens]
        sums_of.append(
            jnp.concatenate(
                [scratch[l, e, pl.ds(l, rows // layers, stride=layers)] for e in range(2)], axis=1
            )
        )
    if mode == "parts":
        for l in range(layers):
            rest[0][l] = sums_of[l]
    else:
        norm_ref, bias_ref, mask_ref, across_ref, act_ref = rest
        for ref in sums:
            sums_of = [value + ref[l] for l, value in enumerate(sums_of)]
        pre = norm_ref[0] * sums_of[0] + norm_ref[1] * sums_of[1] + bias_ref[...]
        act = mask_ref[...].astype(F32).T * pre
        act_ref[...] = act.astype(BF16)
        across_ref[...] = act.T.astype(BF16)


def encode(weight, half, own, near, place, mode, sums=(), norm=None, bias=None, mask=None):
    layers, full = weight.shape[1:]
    tokens = 2 * own.shape[1] // layers
    block = own.shape[2]
    buffer, sems = weight_buffers(weight, half, block)
    _, parts, height, _ = buffer.shape
    rows = height // layers
    latents = parts * rows
    whole = pl.BlockSpec(own.shape, lambda i, s: (0, 0, 0))
    flat = pl.BlockSpec((rows, tokens), lambda i, s: (i, 0))
    split = pl.BlockSpec((layers, rows, tokens), lambda i, s: (0, i, 0))
    in_specs = [pl.BlockSpec(memory_space=pl.ANY)] + [whole] * 2
    in_specs += [flat if value.ndim == 2 else split for value in sums]
    args = [weight, own, near, *sums]
    if mode == "act":
        across = pl.BlockSpec((tokens, rows), lambda i, s: (0, i))
        in_specs += [
            pl.BlockSpec(memory_space=pltpu.SMEM),
            pl.BlockSpec((rows, 1), lambda i, s: (i, 0)),
            across,
        ]
        args += [norm, bias, mask]
        out_specs = (across, flat)
        out_shape = (
            jax.ShapeDtypeStruct((tokens, latents), BF16),
            jax.ShapeDtypeStruct((latents, tokens), BF16),
        )
    else:
        out_specs = split
        out_shape = jax.ShapeDtypeStruct((layers, latents, tokens), F32)
    return pl.pallas_call(
        functools.partial(encode_kernel, half=half, mode=mode, earlier=len(sums)),
        grid_spec=pltpu.PrefetchScalarGridSpec(
            num_scalar_prefetch=1,
            grid=(parts,),
            in_specs=in_specs,
            out_specs=out_specs,
            scratch_shapes=[
                buffer,
                sems,
                pltpu.VMEM((layers * tokens, len(half) * block), BF16),
                pltpu.VMEM((layers, 2, height, tokens // 2), F32),
            ],
        ),
        out_shape=out_shape,
        compiler_params=pltpu.CompilerParams(vmem_limit_bytes=VMEM_BYTES),
        cost_estimate=SMALL,
        name="encode_" + mode,
    )(place, *args)


def rearrange_kernel(place, *refs, halves, count):
    parts = refs[:count]
    outs = refs[-3:-1]
    wide = refs[-1]
    rows, layers, full = parts[0].shape
    chunks = full // LANES
    each = outs[0].shape[2] // len(halves[0]) // LANES
    for p, w_ref in enumerate(parts):
        for c in range(chunks):
            wide[c] = (
                w_ref[:, :, c * LANES:(c + 1) * LANES].reshape(rows * layers, LANES).astype(F32)
            )
        for half, out_ref in zip(halves, outs):
            for i, k in enumerate(half):
                for c in range(each):
                    chunk = (place[0] ^ k) * each + c
                    column = (i * each + c) * LANES
                    for l in range(layers):
                        out_ref[l, p * rows:(p + 1) * rows, column:column + LANES] = wide[
                            chunk, pl.ds(l, rows, stride=layers)
                        ].astype(BF16)


def rearrange(weight, place, halves, runs, run, earlier=()):
    latents, layers, full = weight.shape
    quarter = latents // (2 * runs)
    part = min(64, quarter // 2)
    count = 2
    rows = count * part
    steps = quarter // rows

    def index_of(p):
        return lambda i, s: (((s[1] ^ (2 * run)) * steps + i) * count + p, 0, 0)

    out = pl.BlockSpec((layers, rows, full // 2), lambda i, s: (0, run * steps + i, 0))
    shape = jax.ShapeDtypeStruct((layers, runs * quarter, full // 2), BF16)
    return pl.pallas_call(
        functools.partial(rearrange_kernel, halves=halves, count=count),
        grid_spec=pltpu.PrefetchScalarGridSpec(
            num_scalar_prefetch=1,
            grid=(steps,),
            in_specs=[pl.BlockSpec((part, layers, full), index_of(p)) for p in range(count)]
            + [pl.BlockSpec(memory_space=pl.ANY)] * len(earlier),
            out_specs=(out, out),
            scratch_shapes=[pltpu.VMEM((full // LANES, part * layers, LANES), F32)],
        ),
        out_shape=(shape, shape),
        input_output_aliases={1 + count + i: i for i in range(len(earlier))},
        compiler_params=pltpu.CompilerParams(vmem_limit_bytes=VMEM_BYTES),
        cost_estimate=SMALL,
        name="rearrange",
    )(place, *[weight] * count, *earlier)


def project_kernel(*refs, layers, mode, earlier):
    w_refs = refs[:layers]
    blocks = refs[layers:layers + 2]
    sums = refs[layers + 2:layers + 2 + earlier]
    values = refs[-1]
    rest = refs[layers + 2 + earlier:-1]
    count, height, width = blocks[0].shape
    tokens = height // layers

    @pl.when(pl.program_id(0) == 0)
    def _():
        for e, ref in enumerate(blocks):
            for l in range(layers):
                for i in range(count):
                    values[l, e * tokens:(e + 1) * tokens, i * width:(i + 1) * width] = ref[
                        i, l * tokens:(l + 1) * tokens, :
                    ]

    parts = [
        lax.dot_general(
            w_refs[l][0], values[l], (((1,), (1,)), ((), ())), preferred_element_type=F32
        )
        for l in range(layers)
    ]
    if mode == "sum":
        rest[0][...] = parts[0] + parts[1]
    else:
        total = parts[0] + parts[1]
        for ref in sums:
            total = total + ref[...]
        grad = (rest[0][...].astype(F32).T * total).astype(BF16)
        if len(rest) == 2:
            rest[1][...] = grad
        else:
            own = 2 * pl.program_id(0) < pl.num_programs(0)

            @pl.when(own)
            def _():
                rest[1][...] = grad

            @pl.when(jnp.logical_not(own))
            def _():
                rest[2][...] = grad


def project(matrix, own, near, mode, sums=(), mask=None):
    layers, latents, width = matrix.shape
    tokens = 2 * own.shape[1] // layers
    rows = min(LATENT_ROWS, latents)
    whole = pl.BlockSpec(own.shape, lambda i: (0, 0, 0))
    flat = pl.BlockSpec((rows, tokens), lambda i: (i, 0))
    across = pl.BlockSpec((tokens, rows), lambda i: (0, i))

    def layer(l):
        return pl.BlockSpec((1, rows, width), lambda i: (l, i, 0))

    in_specs = [layer(l) for l in range(layers)] + [whole] * 2
    in_specs += [flat] * len(sums)
    args = [matrix] * layers + [own, near, *sums]
    steps = latents // rows
    out_specs = flat
    out_shape = jax.ShapeDtypeStruct((latents, tokens), BF16 if mode == "grad" else F32)
    if mode == "grad":
        in_specs.append(across)
        args.append(mask)
        if steps > 1:
            middle = steps // 2
            out_specs = (
                pl.BlockSpec((rows, tokens), lambda i: (jnp.minimum(i, middle - 1), 0)),
                pl.BlockSpec((rows, tokens), lambda i: (jnp.maximum(i, middle) - middle, 0)),
            )
            out_shape = (jax.ShapeDtypeStruct((latents // 2, tokens), BF16),) * 2
    out = pl.pallas_call(
        functools.partial(project_kernel, layers=layers, mode=mode, earlier=len(sums)),
        grid=(steps,),
        in_specs=in_specs,
        out_specs=out_specs,
        scratch_shapes=[pltpu.VMEM((layers, tokens, width), BF16)],
        out_shape=out_shape,
        compiler_params=pltpu.CompilerParams(vmem_limit_bytes=VMEM_BYTES),
        cost_estimate=SMALL,
        name="project_" + mode,
    )(*args)
    if mode == "grad" and steps == 1:
        return out[:latents // 2], out[latents // 2:]
    return out


def recon_kernel(act_ref, *refs, parts):
    w_refs = refs[:parts]
    keep_ref = refs[parts]
    send_refs = refs[parts + 1:]
    depth = w_refs[0].shape[1]
    product = None
    for p, w_ref in enumerate(w_refs):
        term = jnp.dot(
            act_ref[:, p * depth:(p + 1) * depth], w_ref[0], preferred_element_type=F32
        )
        product = term if product is None else product + term
    blocks, own, width = keep_ref.shape
    for i in range(blocks):
        keep_ref[i] = product[:own, i * width:(i + 1) * width]
    if len(send_refs) == 1:
        for i in range(blocks):
            send_refs[0][i] = product[own:, i * width:(i + 1) * width].astype(BF16)
    else:
        for pair in range(len(send_refs) // 2):

            @pl.when(pl.program_id(0) == pair)
            def _():
                for i in range(2):
                    send_refs[2 * pair + i][...] = product[
                        own:, i * width:(i + 1) * width
                    ].astype(BF16)


def recon_half(act, matrix, blocks, apart):
    layers, latents, full = matrix.shape
    width = full // blocks
    tokens = act.shape[0] // 2
    parts = 2

    def part(p):
        return pl.BlockSpec((1, latents // parts, 2 * width), lambda i, j: (j, p, i))

    def single(b):
        def index(i, j):
            return jnp.where(i < b // 2, 0, jnp.where(i > b // 2, layers - 1, j)), 0

        return pl.BlockSpec((tokens, width), index)

    out = pl.BlockSpec((2, tokens, width), lambda i, j: (i, j, 0))
    shape = (blocks, layers * tokens, width)
    if apart:
        send_specs = [single(b) for b in range(blocks)]
        send_shapes = [jax.ShapeDtypeStruct(shape[1:], BF16)] * blocks
    else:
        send_specs, send_shapes = [out], [jax.ShapeDtypeStruct(shape, BF16)]
    keep, *send = pl.pallas_call(
        functools.partial(recon_kernel, parts=parts),
        grid=(blocks // 2, layers),
        in_specs=[pl.BlockSpec(act.shape, lambda i, j: (0, 0))] + [part(p) for p in range(parts)],
        out_specs=[out] + send_specs,
        out_shape=[jax.ShapeDtypeStruct(shape, F32)] + send_shapes,
        compiler_params=pltpu.CompilerParams(vmem_limit_bytes=VMEM_BYTES),
        cost_estimate=SMALL,
        name="recon_half",
    )(act, *[matrix] * parts)
    return keep, send


def grad_kernel(place, scale_ref, own_ref, far_ref, *refs, groups, where, sources, scaled):
    value_refs = refs[:sources]
    out_ref, values, left, wide, results, sems, out_sems = refs[sources:]
    pair, pairs = pl.program_id(0), pl.num_programs(0)
    pairs_held, layers, depth, width = values.shape
    tokens = depth // groups
    half = width // 2
    rows = out_ref.shape[0]
    blocks = len(where) // groups
    flat = out_ref.reshape(rows * layers, out_ref.shape[2])

    def copy_of(g, k, l):
        side = (k % 2) ^ place[1]
        source, index = where[g * blocks + k]
        if source is None:
            piece = value_refs[index[0]].at[place[2] ^ g, index[1]]
        elif index < 0:
            piece = value_refs[source]
        else:
            piece = value_refs[source].at[index]
        return pltpu.make_async_copy(
            piece.at[pl.ds(l * tokens, tokens)],
            values.at[
                k // 2, l, pl.ds(g * tokens, tokens), pl.ds(pl.multiple_of(side * half, LANES), half)
            ],
            sems.at[(g * blocks + k) * layers + l],
        )

    def copy_out(turn):
        return pltpu.make_async_copy(
            results.at[lax.rem(turn, 2)],
            flat.at[:, pl.ds(pl.multiple_of((place[0] ^ turn) * width, LANES), width)],
            out_sems.at[lax.rem(turn, 2)],
        )

    @pl.when(pair == 0)
    def _():
        for k in range(blocks):
            for g in range(groups):
                for l in range(layers):
                    copy_of(g, k, l).start()
        near = own_ref.shape[1]
        left[:, :near] = own_ref[...]
        left[:, near:] = far_ref[...]

    for j in range(blocks // 2):

        @pl.when(pair == j)
        def _():
            for b in range(2):
                for g in range(groups):
                    for l in range(layers):
                        copy_of(g, 2 * j + b, l).wait()

    for l in range(layers):
        product = jnp.dot(left[...], values[pair, l], preferred_element_type=F32)
        if scaled:
            product = product * scale_ref[l]
        for c in range(width // LANES):
            wide[c, pl.ds(l, rows, stride=layers)] = product[:, c * LANES:(c + 1) * LANES]

    @pl.when(pair >= 2)
    def _():
        copy_out(pair - 2).wait()

    for c in range(width // LANES):
        results[lax.rem(pair, 2), :, c * LANES:(c + 1) * LANES] = wide[c].astype(BF16)
    copy_out(pair).start()

    @pl.when(pair == pairs - 1)
    def _():
        copy_out(pair - 1).wait()
        copy_out(pair).wait()


def weight_grad(own, far, sources, where, place, scale, scaled, shape):
    rows = far.shape[0]
    layers, full = shape
    groups = lax.axis_size("tok")
    depth = own.shape[1] + far.shape[1]
    blocks = len(where) // groups
    width = full // (blocks // 2)
    anywhere = pl.BlockSpec(memory_space=pl.ANY)
    return pl.pallas_call(
        functools.partial(
            grad_kernel, groups=groups, where=where, sources=len(sources), scaled=scaled
        ),
        grid_spec=pltpu.PrefetchScalarGridSpec(
            num_scalar_prefetch=1,
            grid=(blocks // 2,),
            in_specs=[
                pl.BlockSpec(memory_space=pltpu.SMEM),
                pl.BlockSpec(far.shape, lambda i, s: (0, 0)),
                pl.BlockSpec(far.shape, lambda i, s: (0, 0)),
            ]
            + [anywhere] * len(sources),
            out_specs=anywhere,
            scratch_shapes=[
                pltpu.VMEM((blocks // 2, layers, depth, width), BF16),
                pltpu.VMEM((rows, depth), BF16),
                pltpu.VMEM((width // LANES, rows * layers, LANES), F32),
                pltpu.VMEM((2, rows * layers, width), BF16),
                pltpu.SemaphoreType.DMA((groups * blocks * layers,)),
                pltpu.SemaphoreType.DMA((2,)),
            ],
        ),
        out_shape=jax.ShapeDtypeStruct((rows, layers, full), BF16),
        compiler_params=pltpu.CompilerParams(vmem_limit_bytes=VMEM_BYTES),
        cost_estimate=SMALL,
        name="weight_grad",
    )(place, scale, own, far, *sources)


def per_device(streams, active_mask, enc_weight, enc_bias, dec_weight, dec_bias):
    lat_count = lax.axis_size("lat")
    tok_count = lax.axis_size("tok")
    tok_dev, layers, width_part = streams.shape
    full_width = width_part * lat_count
    tokens = tok_dev * tok_count
    me = lax.axis_index("lat")
    aligned = width_part % LANES == 0
    block_count = lat_count if aligned else 8
    block_width = full_width // block_count
    here = me if aligned else jnp.zeros_like(me)

    own_x = streams.transpose(1, 0, 2).reshape(layers * tok_dev, width_part)
    own_f = own_x.astype(F32).reshape(layers, tok_dev, width_part)
    runs = tok_count // 2
    tok_me = lax.axis_index("tok")
    halves = block_order(block_count)
    spot = jnp.stack([here, tok_me]).astype(jnp.int32)
    place = jnp.stack([here >> 1, here & 1, tok_me]).astype(jnp.int32)

    mask_low = active_mask.astype(BF16)
    mask_far = exchange(run_slices(mask_low, 1, 1), "tok", 1)
    mask = jnp.concatenate([run_slices(mask_low, 0, 1), mask_far], axis=0)
    bias = run_slices(enc_bias.reshape(-1, 1), 0, 0)

    def gather_halves(own, multiply, beside=(), over_tok=False, hops=()):
        blocks, far = gather_features(own, beside, over_tok)
        first = stack([blocks[k] for k in halves[0]])
        first_near = exchange(first, "tok", 1)
        early = [far[4], far[2]] if over_tok else hops[:1]
        sums = multiply(first, after(first_near, *early))
        final = halves[1][-1]
        blocks[final] = after(blocks[final], sums, *hops[1:])
        second = stack([blocks[k] for k in halves[1]])
        near = [first_near, exchange(second, "tok", 1)]
        return [first, second], near, sums, far

    dec_first = rearrange(dec_weight, spot, halves, runs, 0)
    dec_halves = rearrange(dec_weight, spot, halves, runs, 1, dec_first)
    hops = sums_over(jnp.sum(own_f * own_f, axis=(1, 2)), "tok")[-1:]
    hops += sums_over(hops[0], "lat")
    square_sums = hops[-1]
    x_own, x_near, sums, _ = gather_halves(
        own_x,
        lambda own, near: encode(enc_weight, halves[0], own, near, spot, "parts"),
        beside=([*dec_first, mask, bias, hops[0]], [*dec_halves, hops[1]]),
        hops=hops[-2:],
    )
    norm_scale = lax.rsqrt(square_sums / (tokens * full_width) + 1e-06)
    act_across, act = encode(
        enc_weight, halves[1], x_own[1], x_near[1], spot, "act", [sums], norm_scale, bias, mask
    )
    x_all = [lax.all_gather(value, "tok") for value in x_own]
    quarter = act.shape[0] // runs

    bias_part = lax.dynamic_slice_in_dim(dec_bias, me * width_part, width_part, 1)
    keep, send = recon_half(act_across, dec_halves[1], block_count // 2, False)
    cross = keep + exchange(send[0], "tok", 1).astype(F32)
    starts = range(block_count // 2 - 2, -2, -2)
    if aligned:
        bundles = [cross[start:start + 2].astype(BF16) for start in starts]
        act_across = after(act_across, *bundles)
        bundles = [exchange(bundle, "lat", 1) for bundle in bundles]
    keep, send = recon_half(act_across, dec_halves[0], block_count // 2, True)
    send = [exchange(value, "tok", 1) for value in send]
    act_far = exchange(act[quarter:], "tok", 2)
    if aligned:
        pieces = {}
        summed = None
        for start, bundle in zip(starts, bundles):
            if summed is not None:
                bundle = after(bundle, summed)
            low, high = [
                keep[i] + send[i].astype(F32) + bundle[i - start].astype(F32)
                for i in (start, start + 1)
            ]
            received = exchange(high.astype(BF16), "lat", 2)
            summed = low + received.astype(F32)
            if start:
                summed = summed.astype(BF16)
            pieces[2 * start] = summed
        recon = scatter_features(pieces)
    else:
        own = keep + jnp.stack(send).astype(F32)
        whole = jnp.stack([own, cross], axis=1).reshape(block_count, layers * tok_dev, block_width)
        whole = whole.transpose(1, 0, 2).reshape(layers * tok_dev, full_width)
        recon = lax.psum_scatter(whole, "lat", scatter_dimension=1, tiled=True)
    recon = after(recon, act_far, *x_all)

    recon = recon.reshape(layers, tok_dev, width_part) + bias_part[:, None]
    diff = recon - norm_scale[:, None, None] * own_f
    factor = LOSS_SCALE / tokens
    err_low = (diff * factor).astype(BF16).reshape(layers * tok_dev, width_part)
    err_own, err_near, sums, far = gather_halves(
        err_low, lambda own, near: project(dec_halves[0], own, near, "sum"), over_tok=True
    )
    squared = squares(err_own[0], layers) + squares(err_own[1], layers)
    second_near = after(err_near[1], far[6], far[5], squared)
    grad, grad_away = project(dec_halves[1], err_own[1], second_near, "grad", [sums], mask=mask)
    grad_far = exchange(grad_away, "tok", 2)
    error_sums = sums_over(squared, "tok")[-1]
    soon = [k for k in range(block_count) if k not in (3, 7)]
    last = {k: exchange(far[k], "tok", 1) for k in soon}
    grad_far, error_sums, far[3], far[7] = lax.optimization_barrier(
        (grad_far, error_sums, far[3], far[7])
    )

    shape = (layers, full_width)
    spots = {k: (h, i) for h, half in enumerate(halves) for i, k in enumerate(half)}
    order = [spots[k] for k in range(block_count)]
    enc_grad = weight_grad(
        grad, grad_far, x_all, [(None, spot) for spot in order] * tok_count, place,
        norm_scale, True, shape,
    )
    act = after(act, enc_grad)
    for k in (3, 7):
        last[k] = exchange(far[k], "tok", 1)
    where = [(2 * g + h, i) for g in range(2) for h, i in order]
    where += [(4 + g * block_count + k, -1) for g in range(2) for k in range(block_count)]
    sources = err_own + err_near + [group[k] for group in (far, last) for k in range(block_count)]
    dec_grad = weight_grad(act, act_far, sources, where, place, norm_scale, False, shape)
    mean_error = jnp.sum(error_sums) / (factor * factor * tokens * layers * full_width)
    return (enc_grad, dec_grad, mean_error)


def solution(mesh):
    in_specs = (
        P("tok", None, "lat"),
        P("tok", "lat"),
        P("lat", None, None),
        P("lat"),
        P("lat", None, None),
        P(),
    )
    out_specs = (P(("lat", "tok"), None, None), P(("lat", "tok"), None, None), P())
    return jax.shard_map(
        per_device, mesh=mesh, in_specs=in_specs, out_specs=out_specs, check_vma=False
    )
```

```python
import functools

import jax
import jax.numpy as jnp
from jax import lax
from jax.experimental import pallas as pl
from jax.experimental.pallas import tpu as pltpu
from jax.sharding import PartitionSpec as P

LOSS_SCALE = 128.0
LANES = 128
BF16 = jnp.bfloat16
F32 = jnp.float32
LATENT_ROWS = 256
VMEM_BYTES = 63 * 1024 * 1024
SMALL = pl.CostEstimate(flops=1024, bytes_accessed=1024, transcendentals=0)


def exchange(value, axis, mask):
    size = lax.axis_size(axis)
    return lax.ppermute(value, axis, [(i, i ^ mask) for i in range(size)])


def after(value, *others):
    return lax.optimization_barrier((value, *others))[0]


def sum_tokens(value):
    step = 1
    while step < lax.axis_size("tok"):
        value = value + exchange(value, "tok", step)
        step *= 2
    return value


def squares_kernel(ref, out_ref):
    layers, sub, lanes = out_ref.shape
    count, height, width = ref.shape
    tokens = height // layers
    for l in range(layers):
        sums = []
        for i in range(count):
            value = ref[i, l * tokens:(l + 1) * tokens, :].astype(F32)
            value = jnp.sum((value * value).reshape(tokens // sub, sub, width), axis=0)
            total = value[:, :lanes]
            for c in range(1, width // lanes):
                total = total + value[:, c * lanes:(c + 1) * lanes]
            sums.append(total)
        while len(sums) > 1:
            sums = [sums[i] + sums[i + 1] for i in range(0, len(sums), 2)]
        out_ref[l] = sums[0]


def squares(stacked, layers):
    return pl.pallas_call(
        squares_kernel,
        out_shape=jax.ShapeDtypeStruct((layers, 8, LANES), F32),
        compiler_params=pltpu.CompilerParams(vmem_limit_bytes=VMEM_BYTES),
        cost_estimate=SMALL,
        name="squares",
    )(stacked)


def block_order(count):
    return list(range(0, count, 2)), list(range(1, count, 2))


def gather_features(own, beside=(), over_tok=False):
    beside = list(beside)
    count = lax.axis_size("lat")
    if own.shape[1] % LANES:
        blocks = jnp.split(lax.all_gather(own, "lat", axis=1, tiled=True), 8, axis=1)
        return blocks, {k: exchange(blocks[k], "tok", 2) for k in (0, 1) if over_tok}
    direct = {}
    step = count // 2
    while step:
        direct[step] = exchange(own, "lat", step)
        step //= 2
    held = {0: own}
    crossed = {1: direct[1]}
    far = {k: exchange(value, "tok", 2) for k, value in ((0, own), (1, direct[1])) if over_tok}
    early = [value for k, value in direct.items() if k < count // 2]
    early += [far[k] for k in far if k == 0]
    step = count // 2
    while step > 1:
        if beside:
            early += beside.pop(0)
        fresh = {
            k | step: exchange(value, "lat", step) if k else direct[step] for k, value in held.items()
        }
        for k, value in held.items():
            if k | 1 not in crossed:
                crossed[k | 1] = exchange(value, "lat", 1)
                early.append(crossed[k | 1])
        if step < count // 2:
            if over_tok:
                early.append(far[1])
            else:
                crossed[step | 1] = exchange(direct[step], "lat", 1)
                early.append(crossed[step | 1])
        for k, value in fresh.items():
            held[k] = value if k in direct and k < count // 2 else after(value, *early)
        early = []
        step //= 2
    for k, value in held.items():
        if k | 1 not in crossed:
            crossed[k | 1] = exchange(value, "lat", 1)
    held.update(crossed)
    return [held[k] for k in range(count)], far


def stack_kernel(*refs):
    for i, ref in enumerate(refs[:-1]):
        refs[-1][i] = ref[...]


def stack(blocks):
    return pl.pallas_call(
        stack_kernel,
        out_shape=jax.ShapeDtypeStruct((len(blocks), *blocks[0].shape), blocks[0].dtype),
        compiler_params=pltpu.CompilerParams(vmem_limit_bytes=VMEM_BYTES),
        cost_estimate=SMALL,
        name="stack",
    )(*blocks)


def scatter_features(pieces):
    pieces = dict(pieces)
    step = 4
    while step < lax.axis_size("lat"):
        for k in sorted(pieces, reverse=True):
            if k & step:
                sent = pieces.pop(k).astype(BF16)
                pieces[k ^ step] = pieces[k ^ step] + exchange(sent, "lat", step).astype(F32)
        step *= 2
    return pieces[0]


def run_slices(value, mask, axis):
    count = lax.axis_size("tok")
    rows = value.shape[axis] // count
    me = lax.axis_index("tok") ^ mask
    return jnp.concatenate(
        [lax.dynamic_slice_in_dim(value, (me ^ r) * rows, rows, axis) for r in range(0, count, 2)],
        axis=axis,
    )


def weight_copies(place, w_ref, buffer, sems, half):
    latents, layers, full = w_ref.shape
    pairs, parts, height, width = buffer.shape
    block = width // 2
    runs = lax.axis_size("tok") // 2
    quarter = layers * latents // (2 * runs)
    rows = min(height, quarter)
    pieces = height // rows
    flat = w_ref.reshape(latents * layers, full)

    def copies_of(pair, part):
        copies = []
        for piece in range(pieces):
            run, row = divmod(part * height + piece * rows, quarter)
            start = (place[1] ^ (2 * run)) * quarter + row
            for b in range(2):
                column = (place[0] ^ half[2 * pair + b]) * block
                copies.append(
                    pltpu.make_async_copy(
                        flat.at[
                            pl.ds(pl.multiple_of(start, rows), rows),
                            pl.ds(pl.multiple_of(column, LANES), block),
                        ],
                        buffer.at[pair, part, pl.ds(piece * rows, rows), pl.ds(b * block, block)],
                        sems.at[((pair * parts + part) * pieces + piece) * 2 + b],
                    )
                )
        return copies

    return copies_of


def weight_buffers(weight, half, block):
    latents, layers, full = weight.shape
    runs = lax.axis_size("tok") // 2
    quarter = latents // (2 * runs)
    rows = min(LATENT_ROWS, runs * quarter)
    parts = runs * quarter // rows
    pieces = max(1, rows // quarter)
    pairs = len(half) // 2
    return (
        pltpu.VMEM((pairs, parts, layers * rows, 2 * block), BF16),
        pltpu.SemaphoreType.DMA((pairs * parts * pieces * 2,)),
    )


def encode_kernel(place, w_ref, *refs, half, mode, earlier):
    blocks = refs[:2]
    sums = refs[2:2 + earlier]
    buffer, sems, values, scratch = refs[-4:]
    rest = refs[2 + earlier:-4]
    layers = w_ref.shape[1]
    count, height, width = blocks[0].shape
    tokens = height // layers
    pairs, parts, rows, _ = buffer.shape
    step = pl.program_id(0)
    copies_of = weight_copies(place, w_ref, buffer, sems, half)

    @pl.when(step == 0)
    def _():
        for part in range(parts):
            for pair in range(pairs):
                for copy in copies_of(pair, part):
                    copy.start()
        for l in range(layers):
            for e, ref in enumerate(blocks):
                start = (2 * l + e) * tokens
                for i in range(count):
                    values[start:start + tokens, i * width:(i + 1) * width] = ref[
                        i, l * tokens:(l + 1) * tokens, :
                    ]

    for part in range(parts):

        @pl.when(step == part)
        def _():
            for pair in range(pairs):
                for copy in copies_of(pair, part):
                    copy.wait()

    product = None
    for pair in range(pairs):
        term = lax.dot_general(
            buffer[pair, step],
            values[:, pair * 2 * width:(pair + 1) * 2 * width],
            (((1,), (1,)), ((), ())),
            preferred_element_type=F32,
        )
        product = term if product is None else product + term
    sums_of = []
    for l in range(layers):
        for e in range(2):
            scratch[l, e] = product[:, (2 * l + e) * tokens:(2 * l + e + 1) * tokens]
        sums_of.append(
            jnp.concatenate(
                [scratch[l, e, pl.ds(l, rows // layers, stride=layers)] for e in range(2)], axis=1
            )
        )
    if mode == "parts":
        for l in range(layers):
            rest[0][l] = sums_of[l]
    else:
        norm_ref, bias_ref, mask_ref, across_ref, act_ref = rest
        for ref in sums:
            sums_of = [value + ref[l] for l, value in enumerate(sums_of)]
        pre = norm_ref[0] * sums_of[0] + norm_ref[1] * sums_of[1] + bias_ref[...]
        act = mask_ref[...].astype(F32).T * pre
        act_ref[...] = act.astype(BF16)
        across_ref[...] = act.T.astype(BF16)


def encode(weight, half, own, near, place, mode, sums=(), norm=None, bias=None, mask=None):
    layers, full = weight.shape[1:]
    tokens = 2 * own.shape[1] // layers
    block = own.shape[2]
    buffer, sems = weight_buffers(weight, half, block)
    _, parts, height, _ = buffer.shape
    rows = height // layers
    latents = parts * rows
    whole = pl.BlockSpec(own.shape, lambda i, s: (0, 0, 0))
    flat = pl.BlockSpec((rows, tokens), lambda i, s: (i, 0))
    split = pl.BlockSpec((layers, rows, tokens), lambda i, s: (0, i, 0))
    in_specs = [pl.BlockSpec(memory_space=pl.ANY)] + [whole] * 2
    in_specs += [flat if value.ndim == 2 else split for value in sums]
    args = [weight, own, near, *sums]
    if mode == "act":
        across = pl.BlockSpec((tokens, rows), lambda i, s: (0, i))
        in_specs += [
            pl.BlockSpec(memory_space=pltpu.SMEM),
            pl.BlockSpec((rows, 1), lambda i, s: (i, 0)),
            across,
        ]
        args += [norm, bias, mask]
        out_specs = (across, flat)
        out_shape = (
            jax.ShapeDtypeStruct((tokens, latents), BF16),
            jax.ShapeDtypeStruct((latents, tokens), BF16),
        )
    else:
        out_specs = split
        out_shape = jax.ShapeDtypeStruct((layers, latents, tokens), F32)
    return pl.pallas_call(
        functools.partial(encode_kernel, half=half, mode=mode, earlier=len(sums)),
        grid_spec=pltpu.PrefetchScalarGridSpec(
            num_scalar_prefetch=1,
            grid=(parts,),
            in_specs=in_specs,
            out_specs=out_specs,
            scratch_shapes=[
                buffer,
                sems,
                pltpu.VMEM((layers * tokens, len(half) * block), BF16),
                pltpu.VMEM((layers, 2, height, tokens // 2), F32),
            ],
        ),
        out_shape=out_shape,
        compiler_params=pltpu.CompilerParams(vmem_limit_bytes=VMEM_BYTES),
        cost_estimate=SMALL,
        name="encode_" + mode,
    )(place, *args)


def rearrange_kernel(place, *refs, halves, count):
    parts = refs[:count]
    outs = refs[-3:-1]
    wide = refs[-1]
    rows, layers, full = parts[0].shape
    chunks = full // LANES
    each = outs[0].shape[2] // len(halves[0]) // LANES
    for p, w_ref in enumerate(parts):
        for c in range(chunks):
            wide[c] = (
                w_ref[:, :, c * LANES:(c + 1) * LANES].reshape(rows * layers, LANES).astype(F32)
            )
        for half, out_ref in zip(halves, outs):
            for i, k in enumerate(half):
                for c in range(each):
                    chunk = (place[0] ^ k) * each + c
                    column = (i * each + c) * LANES
                    for l in range(layers):
                        out_ref[l, p * rows:(p + 1) * rows, column:column + LANES] = wide[
                            chunk, pl.ds(l, rows, stride=layers)
                        ].astype(BF16)


def rearrange(weight, place, halves, runs, run, earlier=()):
    latents, layers, full = weight.shape
    quarter = latents // (2 * runs)
    part = min(64, quarter // 2)
    count = 2
    rows = count * part
    steps = quarter // rows

    def index_of(p):
        return lambda i, s: (((s[1] ^ (2 * run)) * steps + i) * count + p, 0, 0)

    out = pl.BlockSpec((layers, rows, full // 2), lambda i, s: (0, run * steps + i, 0))
    shape = jax.ShapeDtypeStruct((layers, runs * quarter, full // 2), BF16)
    return pl.pallas_call(
        functools.partial(rearrange_kernel, halves=halves, count=count),
        grid_spec=pltpu.PrefetchScalarGridSpec(
            num_scalar_prefetch=1,
            grid=(steps,),
            in_specs=[pl.BlockSpec((part, layers, full), index_of(p)) for p in range(count)]
            + [pl.BlockSpec(memory_space=pl.ANY)] * len(earlier),
            out_specs=(out, out),
            scratch_shapes=[pltpu.VMEM((full // LANES, part * layers, LANES), F32)],
        ),
        out_shape=(shape, shape),
        input_output_aliases={1 + count + i: i for i in range(len(earlier))},
        compiler_params=pltpu.CompilerParams(vmem_limit_bytes=VMEM_BYTES),
        cost_estimate=SMALL,
        name="rearrange",
    )(place, *[weight] * count, *earlier)


def project_kernel(*refs, layers, mode, earlier):
    w_refs = refs[:layers]
    blocks = refs[layers:layers + 2]
    sums = refs[layers + 2:layers + 2 + earlier]
    values = refs[-1]
    rest = refs[layers + 2 + earlier:-1]
    count, height, width = blocks[0].shape
    tokens = height // layers

    @pl.when(pl.program_id(0) == 0)
    def _():
        for e, ref in enumerate(blocks):
            for l in range(layers):
                for i in range(count):
                    values[l, e * tokens:(e + 1) * tokens, i * width:(i + 1) * width] = ref[
                        i, l * tokens:(l + 1) * tokens, :
                    ]

    parts = [
        lax.dot_general(
            w_refs[l][0], values[l], (((1,), (1,)), ((), ())), preferred_element_type=F32
        )
        for l in range(layers)
    ]
    if mode == "sum":
        rest[0][...] = parts[0] + parts[1]
    else:
        total = parts[0] + parts[1]
        for ref in sums:
            total = total + ref[...]
        grad = (rest[0][...].astype(F32).T * total).astype(BF16)
        if len(rest) == 2:
            rest[1][...] = grad
        else:
            own = 2 * pl.program_id(0) < pl.num_programs(0)

            @pl.when(own)
            def _():
                rest[1][...] = grad

            @pl.when(jnp.logical_not(own))
            def _():
                rest[2][...] = grad


def project(matrix, own, near, mode, sums=(), mask=None):
    layers, latents, width = matrix.shape
    tokens = 2 * own.shape[1] // layers
    rows = min(LATENT_ROWS, latents)
    whole = pl.BlockSpec(own.shape, lambda i: (0, 0, 0))
    flat = pl.BlockSpec((rows, tokens), lambda i: (i, 0))
    across = pl.BlockSpec((tokens, rows), lambda i: (0, i))

    def layer(l):
        return pl.BlockSpec((1, rows, width), lambda i: (l, i, 0))

    in_specs = [layer(l) for l in range(layers)] + [whole] * 2
    in_specs += [flat] * len(sums)
    args = [matrix] * layers + [own, near, *sums]
    steps = latents // rows
    out_specs = flat
    out_shape = jax.ShapeDtypeStruct((latents, tokens), BF16 if mode == "grad" else F32)
    if mode == "grad":
        in_specs.append(across)
        args.append(mask)
        if steps > 1:
            middle = steps // 2
            out_specs = (
                pl.BlockSpec((rows, tokens), lambda i: (jnp.minimum(i, middle - 1), 0)),
                pl.BlockSpec((rows, tokens), lambda i: (jnp.maximum(i, middle) - middle, 0)),
            )
            out_shape = (jax.ShapeDtypeStruct((latents // 2, tokens), BF16),) * 2
    out = pl.pallas_call(
        functools.partial(project_kernel, layers=layers, mode=mode, earlier=len(sums)),
        grid=(steps,),
        in_specs=in_specs,
        out_specs=out_specs,
        scratch_shapes=[pltpu.VMEM((layers, tokens, width), BF16)],
        out_shape=out_shape,
        compiler_params=pltpu.CompilerParams(vmem_limit_bytes=VMEM_BYTES),
        cost_estimate=SMALL,
        name="project_" + mode,
    )(*args)
    if mode == "grad" and steps == 1:
        return out[:latents // 2], out[latents // 2:]
    return out


def recon_kernel(act_ref, *refs, parts):
    w_refs = refs[:parts]
    keep_ref = refs[parts]
    send_refs = refs[parts + 1:]
    depth = w_refs[0].shape[1]
    product = None
    for p, w_ref in enumerate(w_refs):
        term = jnp.dot(
            act_ref[:, p * depth:(p + 1) * depth], w_ref[0], preferred_element_type=F32
        )
        product = term if product is None else product + term
    blocks, own, width = keep_ref.shape
    for i in range(blocks):
        keep_ref[i] = product[:own, i * width:(i + 1) * width]
    if len(send_refs) == 1:
        for i in range(blocks):
            send_refs[0][i] = product[own:, i * width:(i + 1) * width].astype(BF16)
    else:
        for pair in range(len(send_refs) // 2):

            @pl.when(pl.program_id(0) == pair)
            def _():
                for i in range(2):
                    send_refs[2 * pair + i][...] = product[
                        own:, i * width:(i + 1) * width
                    ].astype(BF16)


def recon_half(act, matrix, blocks, apart):
    layers, latents, full = matrix.shape
    width = full // blocks
    tokens = act.shape[0] // 2
    parts = 2

    def part(p):
        return pl.BlockSpec((1, latents // parts, 2 * width), lambda i, j: (j, p, i))

    def single(b):
        def index(i, j):
            return jnp.where(i < b // 2, 0, jnp.where(i > b // 2, layers - 1, j)), 0

        return pl.BlockSpec((tokens, width), index)

    out = pl.BlockSpec((2, tokens, width), lambda i, j: (i, j, 0))
    shape = (blocks, layers * tokens, width)
    if apart:
        send_specs = [single(b) for b in range(blocks)]
        send_shapes = [jax.ShapeDtypeStruct(shape[1:], BF16)] * blocks
    else:
        send_specs, send_shapes = [out], [jax.ShapeDtypeStruct(shape, BF16)]
    keep, *send = pl.pallas_call(
        functools.partial(recon_kernel, parts=parts),
        grid=(blocks // 2, layers),
        in_specs=[pl.BlockSpec(act.shape, lambda i, j: (0, 0))] + [part(p) for p in range(parts)],
        out_specs=[out] + send_specs,
        out_shape=[jax.ShapeDtypeStruct(shape, F32)] + send_shapes,
        compiler_params=pltpu.CompilerParams(vmem_limit_bytes=VMEM_BYTES),
        cost_estimate=SMALL,
        name="recon_half",
    )(act, *[matrix] * parts)
    return keep, send


def grad_kernel(place, scale_ref, own_ref, far_ref, *refs, groups, where, sources, scaled):
    value_refs = refs[:sources]
    out_ref, values, left, wide, results, sems, out_sems = refs[sources:]
    pair, pairs = pl.program_id(0), pl.num_programs(0)
    pairs_held, layers, depth, width = values.shape
    tokens = depth // groups
    half = width // 2
    rows = out_ref.shape[0]
    blocks = len(where) // groups
    flat = out_ref.reshape(rows * layers, out_ref.shape[2])

    def copy_of(g, k, l):
        side = (k % 2) ^ place[1]
        source, index = where[g * blocks + k]
        if source is None:
            piece = value_refs[index[0]].at[place[2] ^ g, index[1]]
        elif index < 0:
            piece = value_refs[source]
        else:
            piece = value_refs[source].at[index]
        return pltpu.make_async_copy(
            piece.at[pl.ds(l * tokens, tokens)],
            values.at[
                k // 2, l, pl.ds(g * tokens, tokens), pl.ds(pl.multiple_of(side * half, LANES), half)
            ],
            sems.at[(g * blocks + k) * layers + l],
        )

    def copy_out(turn):
        return pltpu.make_async_copy(
            results.at[lax.rem(turn, 2)],
            flat.at[:, pl.ds(pl.multiple_of((place[0] ^ turn) * width, LANES), width)],
            out_sems.at[lax.rem(turn, 2)],
        )

    @pl.when(pair == 0)
    def _():
        for k in range(blocks):
            for g in range(groups):
                for l in range(layers):
                    copy_of(g, k, l).start()
        near = own_ref.shape[1]
        left[:, :near] = own_ref[...]
        left[:, near:] = far_ref[...]

    for j in range(blocks // 2):

        @pl.when(pair == j)
        def _():
            for b in range(2):
                for g in range(groups):
                    for l in range(layers):
                        copy_of(g, 2 * j + b, l).wait()

    for l in range(layers):
        product = jnp.dot(left[...], values[pair, l], preferred_element_type=F32)
        if scaled:
            product = product * scale_ref[l]
        for c in range(width // LANES):
            wide[c, pl.ds(l, rows, stride=layers)] = product[:, c * LANES:(c + 1) * LANES]

    @pl.when(pair >= 2)
    def _():
        copy_out(pair - 2).wait()

    for c in range(width // LANES):
        results[lax.rem(pair, 2), :, c * LANES:(c + 1) * LANES] = wide[c].astype(BF16)
    copy_out(pair).start()

    @pl.when(pair == pairs - 1)
    def _():
        copy_out(pair - 1).wait()
        copy_out(pair).wait()


def weight_grad(own, far, sources, where, place, scale, scaled, shape):
    rows = far.shape[0]
    layers, full = shape
    groups = lax.axis_size("tok")
    depth = own.shape[1] + far.shape[1]
    blocks = len(where) // groups
    width = full // (blocks // 2)
    anywhere = pl.BlockSpec(memory_space=pl.ANY)
    return pl.pallas_call(
        functools.partial(
            grad_kernel, groups=groups, where=where, sources=len(sources), scaled=scaled
        ),
        grid_spec=pltpu.PrefetchScalarGridSpec(
            num_scalar_prefetch=1,
            grid=(blocks // 2,),
            in_specs=[
                pl.BlockSpec(memory_space=pltpu.SMEM),
                pl.BlockSpec(far.shape, lambda i, s: (0, 0)),
                pl.BlockSpec(far.shape, lambda i, s: (0, 0)),
            ]
            + [anywhere] * len(sources),
            out_specs=anywhere,
            scratch_shapes=[
                pltpu.VMEM((blocks // 2, layers, depth, width), BF16),
                pltpu.VMEM((rows, depth), BF16),
                pltpu.VMEM((width // LANES, rows * layers, LANES), F32),
                pltpu.VMEM((2, rows * layers, width), BF16),
                pltpu.SemaphoreType.DMA((groups * blocks * layers,)),
                pltpu.SemaphoreType.DMA((2,)),
            ],
        ),
        out_shape=jax.ShapeDtypeStruct((rows, layers, full), BF16),
        compiler_params=pltpu.CompilerParams(vmem_limit_bytes=VMEM_BYTES),
        cost_estimate=pl.CostEstimate(
            flops=4 * rows * depth * layers * full,
            bytes_accessed=8 * rows * layers * full,
            transcendentals=0,
        ),
        name="weight_grad",
    )(place, scale, own, far, *sources)


def per_device(streams, active_mask, enc_weight, enc_bias, dec_weight, dec_bias):
    lat_count = lax.axis_size("lat")
    tok_count = lax.axis_size("tok")
    tok_dev, layers, width_part = streams.shape
    full_width = width_part * lat_count
    tokens = tok_dev * tok_count
    me = lax.axis_index("lat")
    aligned = width_part % LANES == 0
    block_count = lat_count if aligned else 8
    block_width = full_width // block_count
    here = me if aligned else jnp.zeros_like(me)

    own_x = streams.transpose(1, 0, 2).reshape(layers * tok_dev, width_part)
    own_f = own_x.astype(F32).reshape(layers, tok_dev, width_part)
    runs = tok_count // 2
    tok_me = lax.axis_index("tok")
    halves = block_order(block_count)
    spot = jnp.stack([here, tok_me]).astype(jnp.int32)
    place = jnp.stack([here >> 1, here & 1, tok_me]).astype(jnp.int32)

    mask_low = active_mask.astype(BF16)
    mask_far = exchange(run_slices(mask_low, 1, 1), "tok", 1)
    mask = jnp.concatenate([run_slices(mask_low, 0, 1), mask_far], axis=0)
    bias = run_slices(enc_bias.reshape(-1, 1), 0, 0)

    def gather_halves(own, multiply, beside=(), over_tok=False):
        blocks, far = gather_features(own, beside, over_tok)
        first = stack([blocks[k] for k in halves[0]])
        first_near = exchange(first, "tok", 1)
        sums = multiply(first, first_near)
        squared = squares(first, layers)
        early = [sums, squared]
        if over_tok:
            far.update({k: exchange(blocks[k], "tok", 2) for k in (4, 2)})
            early += [far[4], far[2]]
        final = halves[1][-1]
        blocks[final] = after(blocks[final], *early)
        second = stack([blocks[k] for k in halves[1]])
        near = [first_near, exchange(second, "tok", 1)]
        return blocks, [first, second], near, sums, squared, far

    dec_first = rearrange(dec_weight, spot, halves, runs, 0)
    dec_halves = rearrange(dec_weight, spot, halves, runs, 1, dec_first)
    _, x_own, x_near, sums, squared, _ = gather_halves(
        own_x,
        lambda own, near: encode(enc_weight, halves[0], own, near, spot, "parts"),
        beside=([*dec_first, mask, bias], dec_halves),
    )
    square_sums = jnp.sum(sum_tokens(squared + squares(x_own[1], layers)), axis=(1, 2))
    norm_scale = lax.rsqrt(square_sums / (tokens * full_width) + 1e-06)
    act_across, act = encode(
        enc_weight, halves[1], x_own[1], x_near[1], spot, "act", [sums], norm_scale, bias, mask
    )
    x_all = [lax.all_gather(value, "tok") for value in x_own]
    quarter = act.shape[0] // runs

    bias_part = lax.dynamic_slice_in_dim(dec_bias, me * width_part, width_part, 1)
    keep, send = recon_half(act_across, dec_halves[1], block_count // 2, False)
    cross = keep + exchange(send[0], "tok", 1).astype(F32)
    starts = range(block_count // 2 - 2, -2, -2)
    if aligned:
        bundles = [cross[start:start + 2].astype(BF16) for start in starts]
        act_across = after(act_across, *bundles)
        bundles = [exchange(bundle, "lat", 1) for bundle in bundles]
    keep, send = recon_half(act_across, dec_halves[0], block_count // 2, True)
    send = [exchange(value, "tok", 1) for value in send]
    act_far = exchange(act[quarter:], "tok", 2)
    if aligned:
        pieces = {}
        received = None
        for start, bundle in zip(starts, bundles):
            if received is not None:
                bundle = after(bundle, received)
            low, high = [
                keep[i] + send[i].astype(F32) + bundle[i - start].astype(F32)
                for i in (start, start + 1)
            ]
            received = exchange(high.astype(BF16), "lat", 2)
            pieces[2 * start] = low + received.astype(F32)
        recon = scatter_features(pieces)
    else:
        own = keep + jnp.stack(send).astype(F32)
        whole = jnp.stack([own, cross], axis=1).reshape(block_count, layers * tok_dev, block_width)
        whole = whole.transpose(1, 0, 2).reshape(layers * tok_dev, full_width)
        recon = lax.psum_scatter(whole, "lat", scatter_dimension=1, tiled=True)
    recon = after(recon, act_far, *x_all)

    recon = recon.reshape(layers, tok_dev, width_part) + bias_part[:, None]
    diff = recon - norm_scale[:, None, None] * own_f
    factor = LOSS_SCALE / tokens
    err_low = (diff * factor).astype(BF16).reshape(layers * tok_dev, width_part)
    err_blocks, err_own, err_near, sums, squared, far = gather_halves(
        err_low, lambda own, near: project(dec_halves[0], own, near, "sum"), over_tok=True
    )
    far.update({k: exchange(err_blocks[k], "tok", 2) for k in (6, 5)})
    for k in (3, 7):
        far[k] = exchange(far[k ^ 1], "lat", 1) if aligned else exchange(err_blocks[k], "tok", 2)
    grad, grad_away = project(dec_halves[1], err_own[1], err_near[1], "grad", [sums], mask=mask)
    grad_far = exchange(grad_away, "tok", 2)
    error_sums = squared + squares(err_own[1], layers)
    late = (3, 5, 6, 7)
    grad_far, error_sums, *values = lax.optimization_barrier(
        (grad_far, error_sums, *[far[k] for k in late])
    )
    far.update(zip(late, values))
    last = {k: exchange(value, "tok", 1) for k, value in far.items()}

    shape = (layers, full_width)
    spots = {k: (h, i) for h, half in enumerate(halves) for i, k in enumerate(half)}
    order = [spots[k] for k in range(block_count)]
    enc_grad = weight_grad(
        grad, grad_far, x_all, [(None, spot) for spot in order] * tok_count, place,
        norm_scale, True, shape,
    )
    error_sums = error_sums + exchange(error_sums, "tok", 1)
    act, error_sums = lax.optimization_barrier((act, error_sums))
    where = [(2 * g + h, i) for g in range(2) for h, i in order]
    where += [(4 + g * block_count + k, -1) for g in range(2) for k in range(block_count)]
    sources = err_own + err_near + [group[k] for group in (far, last) for k in range(block_count)]
    dec_grad = weight_grad(act, act_far, sources, where, place, norm_scale, False, shape)
    error_sum = jnp.sum(error_sums + exchange(error_sums, "tok", 2))
    mean_error = error_sum / (factor * factor * tokens * layers * full_width)
    return (enc_grad, dec_grad, mean_error)


def solution(mesh):
    in_specs = (
        P("tok", None, "lat"),
        P("tok", "lat"),
        P("lat", None, None),
        P("lat"),
        P("lat", None, None),
        P(),
    )
    out_specs = (P(("lat", "tok"), None, None), P(("lat", "tok"), None, None), P())
    return jax.shard_map(
        per_device, mesh=mesh, in_specs=in_specs, out_specs=out_specs, check_vma=False
    )
```

```python
import functools

import jax
import jax.numpy as jnp
from jax import lax
from jax.experimental import pallas as pl
from jax.experimental.pallas import tpu as pltpu
from jax.sharding import PartitionSpec as P

LOSS_SCALE = 128.0
LANES = 128
BF16 = jnp.bfloat16
F32 = jnp.float32
LATENT_ROWS = 256
VMEM_BYTES = 63 * 1024 * 1024
SMALL = pl.CostEstimate(flops=1024, bytes_accessed=1024, transcendentals=0)


def exchange(value, axis, mask):
    size = lax.axis_size(axis)
    return lax.ppermute(value, axis, [(i, i ^ mask) for i in range(size)])


def after(value, *others):
    return lax.optimization_barrier((value, *others))[0]


def sum_tokens(value):
    step = 1
    while step < lax.axis_size("tok"):
        value = value + exchange(value, "tok", step)
        step *= 2
    return value


def squares_kernel(ref, out_ref):
    layers, sub, lanes = out_ref.shape
    count, height, width = ref.shape
    tokens = height // layers
    for l in range(layers):
        sums = []
        for i in range(count):
            value = ref[i, l * tokens:(l + 1) * tokens, :].astype(F32)
            value = jnp.sum((value * value).reshape(tokens // sub, sub, width), axis=0)
            total = value[:, :lanes]
            for c in range(1, width // lanes):
                total = total + value[:, c * lanes:(c + 1) * lanes]
            sums.append(total)
        while len(sums) > 1:
            sums = [sums[i] + sums[i + 1] for i in range(0, len(sums), 2)]
        out_ref[l] = sums[0]


def squares(stacked, layers):
    return pl.pallas_call(
        squares_kernel,
        out_shape=jax.ShapeDtypeStruct((layers, 8, LANES), F32),
        compiler_params=pltpu.CompilerParams(vmem_limit_bytes=VMEM_BYTES),
        cost_estimate=SMALL,
        name="squares",
    )(stacked)


def block_order(count):
    return list(range(0, count, 2)), list(range(1, count, 2))


def gather_features(own, beside=(), over_tok=False):
    beside = list(beside)
    count = lax.axis_size("lat")
    if own.shape[1] % LANES:
        blocks = jnp.split(lax.all_gather(own, "lat", axis=1, tiled=True), 8, axis=1)
        return blocks, {k: exchange(blocks[k], "tok", 2) for k in (0, 1) if over_tok}
    direct = {}
    step = count // 2
    while step:
        direct[step] = exchange(own, "lat", step)
        step //= 2
    held = {0: own}
    crossed = {1: direct[1]}
    far = {k: exchange(value, "tok", 2) for k, value in ((0, own), (1, direct[1])) if over_tok}
    early = [value for k, value in direct.items() if k < count // 2]
    early += [far[k] for k in far if k == 0]
    step = count // 2
    while step > 1:
        if beside:
            early += beside.pop(0)
        fresh = {
            k | step: exchange(value, "lat", step) if k else direct[step] for k, value in held.items()
        }
        for k, value in held.items():
            if k | 1 not in crossed:
                crossed[k | 1] = exchange(value, "lat", 1)
                early.append(crossed[k | 1])
        if step < count // 2:
            if over_tok:
                early.append(far[1])
            else:
                crossed[step | 1] = exchange(direct[step], "lat", 1)
                early.append(crossed[step | 1])
        for k, value in fresh.items():
            held[k] = value if k in direct and k < count // 2 else after(value, *early)
        early = []
        step //= 2
    for k, value in held.items():
        if k | 1 not in crossed:
            crossed[k | 1] = exchange(value, "lat", 1)
    held.update(crossed)
    return [held[k] for k in range(count)], far


def stack_kernel(*refs):
    for i, ref in enumerate(refs[:-1]):
        refs[-1][i] = ref[...]


def stack(blocks):
    return pl.pallas_call(
        stack_kernel,
        out_shape=jax.ShapeDtypeStruct((len(blocks), *blocks[0].shape), blocks[0].dtype),
        compiler_params=pltpu.CompilerParams(vmem_limit_bytes=VMEM_BYTES),
        cost_estimate=SMALL,
        name="stack",
    )(*blocks)


def scatter_features(pieces):
    pieces = dict(pieces)
    step = 4
    while step < lax.axis_size("lat"):
        for k in sorted(pieces, reverse=True):
            if k & step:
                sent = pieces.pop(k).astype(BF16)
                pieces[k ^ step] = pieces[k ^ step] + exchange(sent, "lat", step).astype(F32)
        step *= 2
    return pieces[0]


def run_slices(value, mask, axis):
    count = lax.axis_size("tok")
    rows = value.shape[axis] // count
    me = lax.axis_index("tok") ^ mask
    return jnp.concatenate(
        [lax.dynamic_slice_in_dim(value, (me ^ r) * rows, rows, axis) for r in range(0, count, 2)],
        axis=axis,
    )


def weight_copies(place, w_ref, buffer, sems, half):
    latents, layers, full = w_ref.shape
    pairs, parts, height, width = buffer.shape
    block = width // 2
    runs = lax.axis_size("tok") // 2
    quarter = layers * latents // (2 * runs)
    rows = min(height, quarter)
    pieces = height // rows
    flat = w_ref.reshape(latents * layers, full)

    def copies_of(pair, part):
        copies = []
        for piece in range(pieces):
            run, row = divmod(part * height + piece * rows, quarter)
            start = (place[1] ^ (2 * run)) * quarter + row
            for b in range(2):
                column = (place[0] ^ half[2 * pair + b]) * block
                copies.append(
                    pltpu.make_async_copy(
                        flat.at[
                            pl.ds(pl.multiple_of(start, rows), rows),
                            pl.ds(pl.multiple_of(column, LANES), block),
                        ],
                        buffer.at[pair, part, pl.ds(piece * rows, rows), pl.ds(b * block, block)],
                        sems.at[((pair * parts + part) * pieces + piece) * 2 + b],
                    )
                )
        return copies

    return copies_of


def weight_buffers(weight, half, block):
    latents, layers, full = weight.shape
    runs = lax.axis_size("tok") // 2
    quarter = latents // (2 * runs)
    rows = min(LATENT_ROWS, runs * quarter)
    parts = runs * quarter // rows
    pieces = max(1, rows // quarter)
    pairs = len(half) // 2
    return (
        pltpu.VMEM((pairs, parts, layers * rows, 2 * block), BF16),
        pltpu.SemaphoreType.DMA((pairs * parts * pieces * 2,)),
    )


def encode_kernel(place, w_ref, *refs, half, mode, earlier):
    blocks = refs[:2]
    sums = refs[2:2 + earlier]
    buffer, sems, values, scratch = refs[-4:]
    rest = refs[2 + earlier:-4]
    layers = w_ref.shape[1]
    count, height, width = blocks[0].shape
    tokens = height // layers
    pairs, parts, rows, _ = buffer.shape
    step = pl.program_id(0)
    copies_of = weight_copies(place, w_ref, buffer, sems, half)

    @pl.when(step == 0)
    def _():
        for part in range(parts):
            for pair in range(pairs):
                for copy in copies_of(pair, part):
                    copy.start()
        for l in range(layers):
            for e, ref in enumerate(blocks):
                start = (2 * l + e) * tokens
                for i in range(count):
                    values[start:start + tokens, i * width:(i + 1) * width] = ref[
                        i, l * tokens:(l + 1) * tokens, :
                    ]

    for part in range(parts):

        @pl.when(step == part)
        def _():
            for pair in range(pairs):
                for copy in copies_of(pair, part):
                    copy.wait()

    product = None
    for pair in range(pairs):
        term = lax.dot_general(
            buffer[pair, step],
            values[:, pair * 2 * width:(pair + 1) * 2 * width],
            (((1,), (1,)), ((), ())),
            preferred_element_type=F32,
        )
        product = term if product is None else product + term
    sums_of = []
    for l in range(layers):
        for e in range(2):
            scratch[l, e] = product[:, (2 * l + e) * tokens:(2 * l + e + 1) * tokens]
        sums_of.append(
            jnp.concatenate(
                [scratch[l, e, pl.ds(l, rows // layers, stride=layers)] for e in range(2)], axis=1
            )
        )
    if mode == "parts":
        for l in range(layers):
            rest[0][l] = sums_of[l]
    else:
        norm_ref, bias_ref, mask_ref, across_ref, act_ref = rest
        for ref in sums:
            sums_of = [value + ref[l] for l, value in enumerate(sums_of)]
        pre = norm_ref[0] * sums_of[0] + norm_ref[1] * sums_of[1] + bias_ref[...]
        act = mask_ref[...].astype(F32).T * pre
        act_ref[...] = act.astype(BF16)
        across_ref[...] = act.T.astype(BF16)


def encode(weight, half, own, near, place, mode, sums=(), norm=None, bias=None, mask=None):
    layers, full = weight.shape[1:]
    tokens = 2 * own.shape[1] // layers
    block = own.shape[2]
    buffer, sems = weight_buffers(weight, half, block)
    _, parts, height, _ = buffer.shape
    rows = height // layers
    latents = parts * rows
    whole = pl.BlockSpec(own.shape, lambda i, s: (0, 0, 0))
    flat = pl.BlockSpec((rows, tokens), lambda i, s: (i, 0))
    split = pl.BlockSpec((layers, rows, tokens), lambda i, s: (0, i, 0))
    in_specs = [pl.BlockSpec(memory_space=pl.ANY)] + [whole] * 2
    in_specs += [flat if value.ndim == 2 else split for value in sums]
    args = [weight, own, near, *sums]
    if mode == "act":
        across = pl.BlockSpec((tokens, rows), lambda i, s: (0, i))
        in_specs += [
            pl.BlockSpec(memory_space=pltpu.SMEM),
            pl.BlockSpec((rows, 1), lambda i, s: (i, 0)),
            across,
        ]
        args += [norm, bias, mask]
        out_specs = (across, flat)
        out_shape = (
            jax.ShapeDtypeStruct((tokens, latents), BF16),
            jax.ShapeDtypeStruct((latents, tokens), BF16),
        )
    else:
        out_specs = split
        out_shape = jax.ShapeDtypeStruct((layers, latents, tokens), F32)
    return pl.pallas_call(
        functools.partial(encode_kernel, half=half, mode=mode, earlier=len(sums)),
        grid_spec=pltpu.PrefetchScalarGridSpec(
            num_scalar_prefetch=1,
            grid=(parts,),
            in_specs=in_specs,
            out_specs=out_specs,
            scratch_shapes=[
                buffer,
                sems,
                pltpu.VMEM((layers * tokens, len(half) * block), BF16),
                pltpu.VMEM((layers, 2, height, tokens // 2), F32),
            ],
        ),
        out_shape=out_shape,
        compiler_params=pltpu.CompilerParams(vmem_limit_bytes=VMEM_BYTES),
        cost_estimate=SMALL,
        name="encode_" + mode,
    )(place, *args)


def rearrange_kernel(place, *refs, halves, count):
    parts = refs[:count]
    outs = refs[-3:-1]
    wide = refs[-1]
    rows, layers, full = parts[0].shape
    chunks = full // LANES
    each = outs[0].shape[2] // len(halves[0]) // LANES
    for p, w_ref in enumerate(parts):
        for c in range(chunks):
            wide[c] = (
                w_ref[:, :, c * LANES:(c + 1) * LANES].reshape(rows * layers, LANES).astype(F32)
            )
        for half, out_ref in zip(halves, outs):
            for i, k in enumerate(half):
                for c in range(each):
                    chunk = (place[0] ^ k) * each + c
                    column = (i * each + c) * LANES
                    for l in range(layers):
                        out_ref[l, p * rows:(p + 1) * rows, column:column + LANES] = wide[
                            chunk, pl.ds(l, rows, stride=layers)
                        ].astype(BF16)


def rearrange(weight, place, halves, runs, run, earlier=()):
    latents, layers, full = weight.shape
    quarter = latents // (2 * runs)
    part = min(64, quarter // 2)
    count = 2
    rows = count * part
    steps = quarter // rows

    def index_of(p):
        return lambda i, s: (((s[1] ^ (2 * run)) * steps + i) * count + p, 0, 0)

    out = pl.BlockSpec((layers, rows, full // 2), lambda i, s: (0, run * steps + i, 0))
    shape = jax.ShapeDtypeStruct((layers, runs * quarter, full // 2), BF16)
    return pl.pallas_call(
        functools.partial(rearrange_kernel, halves=halves, count=count),
        grid_spec=pltpu.PrefetchScalarGridSpec(
            num_scalar_prefetch=1,
            grid=(steps,),
            in_specs=[pl.BlockSpec((part, layers, full), index_of(p)) for p in range(count)]
            + [pl.BlockSpec(memory_space=pl.ANY)] * len(earlier),
            out_specs=(out, out),
            scratch_shapes=[pltpu.VMEM((full // LANES, part * layers, LANES), F32)],
        ),
        out_shape=(shape, shape),
        input_output_aliases={1 + count + i: i for i in range(len(earlier))},
        compiler_params=pltpu.CompilerParams(vmem_limit_bytes=VMEM_BYTES),
        cost_estimate=SMALL,
        name="rearrange",
    )(place, *[weight] * count, *earlier)


def project_kernel(*refs, layers, mode, earlier):
    w_refs = refs[:layers]
    blocks = refs[layers:layers + 2]
    sums = refs[layers + 2:layers + 2 + earlier]
    values = refs[-1]
    rest = refs[layers + 2 + earlier:-1]
    count, height, width = blocks[0].shape
    tokens = height // layers

    @pl.when(pl.program_id(0) == 0)
    def _():
        for e, ref in enumerate(blocks):
            for l in range(layers):
                for i in range(count):
                    values[l, e * tokens:(e + 1) * tokens, i * width:(i + 1) * width] = ref[
                        i, l * tokens:(l + 1) * tokens, :
                    ]

    parts = [
        lax.dot_general(
            w_refs[l][0], values[l], (((1,), (1,)), ((), ())), preferred_element_type=F32
        )
        for l in range(layers)
    ]
    if mode == "sum":
        rest[0][...] = parts[0] + parts[1]
    else:
        total = parts[0] + parts[1]
        for ref in sums:
            total = total + ref[...]
        grad = (rest[0][...].astype(F32).T * total).astype(BF16)
        if len(rest) == 2:
            rest[1][...] = grad
        else:
            own = 2 * pl.program_id(0) < pl.num_programs(0)

            @pl.when(own)
            def _():
                rest[1][...] = grad

            @pl.when(jnp.logical_not(own))
            def _():
                rest[2][...] = grad


def project(matrix, own, near, mode, sums=(), mask=None):
    layers, latents, width = matrix.shape
    tokens = 2 * own.shape[1] // layers
    rows = min(LATENT_ROWS, latents)
    whole = pl.BlockSpec(own.shape, lambda i: (0, 0, 0))
    flat = pl.BlockSpec((rows, tokens), lambda i: (i, 0))
    across = pl.BlockSpec((tokens, rows), lambda i: (0, i))

    def layer(l):
        return pl.BlockSpec((1, rows, width), lambda i: (l, i, 0))

    in_specs = [layer(l) for l in range(layers)] + [whole] * 2
    in_specs += [flat] * len(sums)
    args = [matrix] * layers + [own, near, *sums]
    steps = latents // rows
    out_specs = flat
    out_shape = jax.ShapeDtypeStruct((latents, tokens), BF16 if mode == "grad" else F32)
    if mode == "grad":
        in_specs.append(across)
        args.append(mask)
        if steps > 1:
            middle = steps // 2
            out_specs = (
                pl.BlockSpec((rows, tokens), lambda i: (jnp.minimum(i, middle - 1), 0)),
                pl.BlockSpec((rows, tokens), lambda i: (jnp.maximum(i, middle) - middle, 0)),
            )
            out_shape = (jax.ShapeDtypeStruct((latents // 2, tokens), BF16),) * 2
    out = pl.pallas_call(
        functools.partial(project_kernel, layers=layers, mode=mode, earlier=len(sums)),
        grid=(steps,),
        in_specs=in_specs,
        out_specs=out_specs,
        scratch_shapes=[pltpu.VMEM((layers, tokens, width), BF16)],
        out_shape=out_shape,
        compiler_params=pltpu.CompilerParams(vmem_limit_bytes=VMEM_BYTES),
        cost_estimate=SMALL,
        name="project_" + mode,
    )(*args)
    if mode == "grad" and steps == 1:
        return out[:latents // 2], out[latents // 2:]
    return out


def recon_kernel(act_ref, *refs, parts):
    w_refs = refs[:parts]
    keep_ref = refs[parts]
    send_refs = refs[parts + 1:]
    depth = w_refs[0].shape[1]
    product = None
    for p, w_ref in enumerate(w_refs):
        term = jnp.dot(
            act_ref[:, p * depth:(p + 1) * depth], w_ref[0], preferred_element_type=F32
        )
        product = term if product is None else product + term
    blocks, own, width = keep_ref.shape
    for i in range(blocks):
        keep_ref[i] = product[:own, i * width:(i + 1) * width]
    if len(send_refs) == 1:
        for i in range(blocks):
            send_refs[0][i] = product[own:, i * width:(i + 1) * width].astype(BF16)
    else:
        for pair in range(len(send_refs) // 2):

            @pl.when(pl.program_id(0) == pair)
            def _():
                for i in range(2):
                    send_refs[2 * pair + i][...] = product[
                        own:, i * width:(i + 1) * width
                    ].astype(BF16)


def recon_half(act, matrix, blocks, apart):
    layers, latents, full = matrix.shape
    width = full // blocks
    tokens = act.shape[0] // 2
    parts = 2

    def part(p):
        return pl.BlockSpec((1, latents // parts, 2 * width), lambda i, j: (j, p, i))

    def single(b):
        def index(i, j):
            return jnp.where(i < b // 2, 0, jnp.where(i > b // 2, layers - 1, j)), 0

        return pl.BlockSpec((tokens, width), index)

    out = pl.BlockSpec((2, tokens, width), lambda i, j: (i, j, 0))
    shape = (blocks, layers * tokens, width)
    if apart:
        send_specs = [single(b) for b in range(blocks)]
        send_shapes = [jax.ShapeDtypeStruct(shape[1:], BF16)] * blocks
    else:
        send_specs, send_shapes = [out], [jax.ShapeDtypeStruct(shape, BF16)]
    keep, *send = pl.pallas_call(
        functools.partial(recon_kernel, parts=parts),
        grid=(blocks // 2, layers),
        in_specs=[pl.BlockSpec(act.shape, lambda i, j: (0, 0))] + [part(p) for p in range(parts)],
        out_specs=[out] + send_specs,
        out_shape=[jax.ShapeDtypeStruct(shape, F32)] + send_shapes,
        compiler_params=pltpu.CompilerParams(vmem_limit_bytes=VMEM_BYTES),
        cost_estimate=SMALL,
        name="recon_half",
    )(act, *[matrix] * parts)
    return keep, send


def grad_kernel(place, scale_ref, own_ref, far_ref, *refs, groups, where, sources, scaled):
    value_refs = refs[:sources]
    out_ref, values, left, wide, results, sems, out_sems = refs[sources:]
    pair, pairs = pl.program_id(0), pl.num_programs(0)
    pairs_held, layers, depth, width = values.shape
    tokens = depth // groups
    half = width // 2
    rows = out_ref.shape[0]
    blocks = len(where) // groups
    flat = out_ref.reshape(rows * layers, out_ref.shape[2])

    def copy_of(g, k, l):
        side = (k % 2) ^ place[1]
        source, index = where[g * blocks + k]
        if source is None:
            piece = value_refs[index[0]].at[place[2] ^ g, index[1]]
        elif index < 0:
            piece = value_refs[source]
        else:
            piece = value_refs[source].at[index]
        return pltpu.make_async_copy(
            piece.at[pl.ds(l * tokens, tokens)],
            values.at[
                k // 2, l, pl.ds(g * tokens, tokens), pl.ds(pl.multiple_of(side * half, LANES), half)
            ],
            sems.at[(g * blocks + k) * layers + l],
        )

    def copies_out(turn):
        part = rows * layers // 2
        return [
            pltpu.make_async_copy(
                results.at[lax.rem(turn, 2), pl.ds(i * part, part)],
                flat.at[
                    pl.ds(i * part, part),
                    pl.ds(pl.multiple_of((place[0] ^ turn) * width, LANES), width),
                ],
                out_sems.at[2 * lax.rem(turn, 2) + i],
            )
            for i in range(2)
        ]

    @pl.when(pair == 0)
    def _():
        for k in range(blocks):
            for g in range(groups):
                for l in range(layers):
                    copy_of(g, k, l).start()
        near = own_ref.shape[1]
        left[:, :near] = own_ref[...]
        left[:, near:] = far_ref[...]

    for j in range(blocks // 2):

        @pl.when(pair == j)
        def _():
            for b in range(2):
                for g in range(groups):
                    for l in range(layers):
                        copy_of(g, 2 * j + b, l).wait()

    for l in range(layers):
        product = jnp.dot(left[...], values[pair, l], preferred_element_type=F32)
        if scaled:
            product = product * scale_ref[l]
        for c in range(width // LANES):
            wide[c, pl.ds(l, rows, stride=layers)] = product[:, c * LANES:(c + 1) * LANES]

    @pl.when(pair >= 2)
    def _():
        for copy in copies_out(pair - 2):
            copy.wait()

    for c in range(width // LANES):
        results[lax.rem(pair, 2), :, c * LANES:(c + 1) * LANES] = wide[c].astype(BF16)
    for copy in copies_out(pair):
        copy.start()

    @pl.when(pair == pairs - 1)
    def _():
        for copy in copies_out(pair - 1) + copies_out(pair):
            copy.wait()


def weight_grad(own, far, sources, where, place, scale, scaled, shape):
    rows = far.shape[0]
    layers, full = shape
    groups = lax.axis_size("tok")
    depth = own.shape[1] + far.shape[1]
    blocks = len(where) // groups
    width = full // (blocks // 2)
    anywhere = pl.BlockSpec(memory_space=pl.ANY)
    return pl.pallas_call(
        functools.partial(
            grad_kernel, groups=groups, where=where, sources=len(sources), scaled=scaled
        ),
        grid_spec=pltpu.PrefetchScalarGridSpec(
            num_scalar_prefetch=1,
            grid=(blocks // 2,),
            in_specs=[
                pl.BlockSpec(memory_space=pltpu.SMEM),
                pl.BlockSpec(far.shape, lambda i, s: (0, 0)),
                pl.BlockSpec(far.shape, lambda i, s: (0, 0)),
            ]
            + [anywhere] * len(sources),
            out_specs=anywhere,
            scratch_shapes=[
                pltpu.VMEM((blocks // 2, layers, depth, width), BF16),
                pltpu.VMEM((rows, depth), BF16),
                pltpu.VMEM((width // LANES, rows * layers, LANES), F32),
                pltpu.VMEM((2, rows * layers, width), BF16),
                pltpu.SemaphoreType.DMA((groups * blocks * layers,)),
                pltpu.SemaphoreType.DMA((4,)),
            ],
        ),
        out_shape=jax.ShapeDtypeStruct((rows, layers, full), BF16),
        compiler_params=pltpu.CompilerParams(vmem_limit_bytes=VMEM_BYTES),
        cost_estimate=pl.CostEstimate(
            flops=4 * rows * depth * layers * full,
            bytes_accessed=8 * rows * layers * full,
            transcendentals=0,
        ),
        name="weight_grad",
    )(place, scale, own, far, *sources)


def per_device(streams, active_mask, enc_weight, enc_bias, dec_weight, dec_bias):
    lat_count = lax.axis_size("lat")
    tok_count = lax.axis_size("tok")
    tok_dev, layers, width_part = streams.shape
    full_width = width_part * lat_count
    tokens = tok_dev * tok_count
    me = lax.axis_index("lat")
    aligned = width_part % LANES == 0
    block_count = lat_count if aligned else 8
    block_width = full_width // block_count
    here = me if aligned else jnp.zeros_like(me)

    own_x = streams.transpose(1, 0, 2).reshape(layers * tok_dev, width_part)
    own_f = own_x.astype(F32).reshape(layers, tok_dev, width_part)
    runs = tok_count // 2
    tok_me = lax.axis_index("tok")
    halves = block_order(block_count)
    spot = jnp.stack([here, tok_me]).astype(jnp.int32)
    place = jnp.stack([here >> 1, here & 1, tok_me]).astype(jnp.int32)

    mask_low = active_mask.astype(BF16)
    mask_far = exchange(run_slices(mask_low, 1, 1), "tok", 1)
    mask = jnp.concatenate([run_slices(mask_low, 0, 1), mask_far], axis=0)
    bias = run_slices(enc_bias.reshape(-1, 1), 0, 0)

    def gather_halves(own, multiply, beside=(), over_tok=False):
        blocks, far = gather_features(own, beside, over_tok)
        first = stack([blocks[k] for k in halves[0]])
        first_near = exchange(first, "tok", 1)
        sums = multiply(first, first_near)
        squared = squares(first, layers)
        early = [sums, squared]
        if over_tok:
            far.update({k: exchange(blocks[k], "tok", 2) for k in (4, 2)})
            early += [far[4], far[2]]
        final = halves[1][-1]
        blocks[final] = after(blocks[final], *early)
        second = stack([blocks[k] for k in halves[1]])
        near = [first_near, exchange(second, "tok", 1)]
        return blocks, [first, second], near, sums, squared, far

    dec_first = rearrange(dec_weight, spot, halves, runs, 0)
    dec_halves = rearrange(dec_weight, spot, halves, runs, 1, dec_first)
    _, x_own, x_near, sums, squared, _ = gather_halves(
        own_x,
        lambda own, near: encode(enc_weight, halves[0], own, near, spot, "parts"),
        beside=([*dec_first, mask, bias], dec_halves),
    )
    square_sums = jnp.sum(sum_tokens(squared + squares(x_own[1], layers)), axis=(1, 2))
    norm_scale = lax.rsqrt(square_sums / (tokens * full_width) + 1e-06)
    act_across, act = encode(
        enc_weight, halves[1], x_own[1], x_near[1], spot, "act", [sums], norm_scale, bias, mask
    )
    x_all = [lax.all_gather(value, "tok") for value in x_own]
    quarter = act.shape[0] // runs

    bias_part = lax.dynamic_slice_in_dim(dec_bias, me * width_part, width_part, 1)
    keep, send = recon_half(act_across, dec_halves[1], block_count // 2, False)
    cross = keep + exchange(send[0], "tok", 1).astype(F32)
    starts = range(block_count // 2 - 2, -2, -2)
    if aligned:
        bundles = [cross[start:start + 2].astype(BF16) for start in starts]
        act_across = after(act_across, *bundles)
        bundles = [exchange(bundle, "lat", 1) for bundle in bundles]
    keep, send = recon_half(act_across, dec_halves[0], block_count // 2, True)
    send = [exchange(value, "tok", 1) for value in send]
    act_far = exchange(act[quarter:], "tok", 2)
    if aligned:
        pieces = {}
        received = None
        for start, bundle in zip(starts, bundles):
            if received is not None:
                bundle = after(bundle, received)
            low, high = [
                keep[i] + send[i].astype(F32) + bundle[i - start].astype(F32)
                for i in (start, start + 1)
            ]
            received = exchange(high.astype(BF16), "lat", 2)
            pieces[2 * start] = low + received.astype(F32)
        recon = scatter_features(pieces)
    else:
        own = keep + jnp.stack(send).astype(F32)
        whole = jnp.stack([own, cross], axis=1).reshape(block_count, layers * tok_dev, block_width)
        whole = whole.transpose(1, 0, 2).reshape(layers * tok_dev, full_width)
        recon = lax.psum_scatter(whole, "lat", scatter_dimension=1, tiled=True)
    recon = after(recon, act_far, *x_all)

    recon = recon.reshape(layers, tok_dev, width_part) + bias_part[:, None]
    diff = recon - norm_scale[:, None, None] * own_f
    factor = LOSS_SCALE / tokens
    err_low = (diff * factor).astype(BF16).reshape(layers * tok_dev, width_part)
    err_blocks, err_own, err_near, sums, squared, far = gather_halves(
        err_low, lambda own, near: project(dec_halves[0], own, near, "sum"), over_tok=True
    )
    far.update({k: exchange(err_blocks[k], "tok", 2) for k in (6, 5)})
    grad, grad_away = project(dec_halves[1], err_own[1], err_near[1], "grad", [sums], mask=mask)
    grad_far = exchange(grad_away, "tok", 2)
    for k, value in ((3, far[2]), (7, after(far[6], grad_away))):
        far[k] = exchange(value, "lat", 1) if aligned else exchange(err_blocks[k], "tok", 2)
    error_sums = squared + squares(err_own[1], layers)
    late = (3, 5, 6, 7)
    grad_far, error_sums, *values = lax.optimization_barrier(
        (grad_far, error_sums, *[far[k] for k in late])
    )
    far.update(zip(late, values))
    last = {k: exchange(value, "tok", 1) for k, value in far.items()}

    shape = (layers, full_width)
    spots = {k: (h, i) for h, half in enumerate(halves) for i, k in enumerate(half)}
    order = [spots[k] for k in range(block_count)]
    enc_grad = weight_grad(
        grad, grad_far, x_all, [(None, spot) for spot in order] * tok_count, place,
        norm_scale, True, shape,
    )
    error_sums = error_sums + exchange(error_sums, "tok", 1)
    act, error_sums = lax.optimization_barrier((act, error_sums))
    where = [(2 * g + h, i) for g in range(2) for h, i in order]
    where += [(4 + g * block_count + k, -1) for g in range(2) for k in range(block_count)]
    sources = err_own + err_near + [group[k] for group in (far, last) for k in range(block_count)]
    dec_grad = weight_grad(act, act_far, sources, where, place, norm_scale, False, shape)
    error_sum = jnp.sum(error_sums + exchange(error_sums, "tok", 2))
    mean_error = error_sum / (factor * factor * tokens * layers * full_width)
    return (enc_grad, dec_grad, mean_error)


def solution(mesh):
    in_specs = (
        P("tok", None, "lat"),
        P("tok", "lat"),
        P("lat", None, None),
        P("lat"),
        P("lat", None, None),
        P(),
    )
    out_specs = (P(("lat", "tok"), None, None), P(("lat", "tok"), None, None), P())
    return jax.shard_map(
        per_device, mesh=mesh, in_specs=in_specs, out_specs=out_specs, check_vma=False
    )
```

```python
import functools

import jax
import jax.numpy as jnp
from jax import lax
from jax.experimental import pallas as pl
from jax.experimental.pallas import tpu as pltpu
from jax.sharding import PartitionSpec as P

LOSS_SCALE = 128.0
LANES = 128
BF16 = jnp.bfloat16
F32 = jnp.float32
LATENT_ROWS = 256
VMEM_BYTES = 63 * 1024 * 1024
SMALL = pl.CostEstimate(flops=1024, bytes_accessed=1024, transcendentals=0)


def exchange(value, axis, mask):
    size = lax.axis_size(axis)
    return lax.ppermute(value, axis, [(i, i ^ mask) for i in range(size)])


def after(value, *others):
    return lax.optimization_barrier((value, *others))[0]


def sum_tokens(value):
    sums = [value] + [exchange(value, "tok", g) for g in range(1, lax.axis_size("tok"))]
    while len(sums) > 1:
        sums = [sums[i] + sums[i + 1] for i in range(0, len(sums), 2)]
    return sums[0]


def squares_kernel(ref, out_ref):
    layers, sub, lanes = out_ref.shape
    count, height, width = ref.shape
    tokens = height // layers
    for l in range(layers):
        sums = []
        for i in range(count):
            value = ref[i, l * tokens:(l + 1) * tokens, :].astype(F32)
            value = jnp.sum((value * value).reshape(tokens // sub, sub, width), axis=0)
            total = value[:, :lanes]
            for c in range(1, width // lanes):
                total = total + value[:, c * lanes:(c + 1) * lanes]
            sums.append(total)
        while len(sums) > 1:
            sums = [sums[i] + sums[i + 1] for i in range(0, len(sums), 2)]
        out_ref[l] = sums[0]


def squares(stacked, layers):
    return pl.pallas_call(
        squares_kernel,
        out_shape=jax.ShapeDtypeStruct((layers, 8, LANES), F32),
        compiler_params=pltpu.CompilerParams(vmem_limit_bytes=VMEM_BYTES),
        cost_estimate=SMALL,
        name="squares",
    )(stacked)


def block_order(count):
    return list(range(0, count, 2)), list(range(1, count, 2))


def gather_features(own, beside=(), over_tok=False):
    beside = list(beside)
    count = lax.axis_size("lat")
    if own.shape[1] % LANES:
        blocks = jnp.split(lax.all_gather(own, "lat", axis=1, tiled=True), 8, axis=1)
        return blocks, {k: exchange(blocks[k], "tok", 2) for k in (0, 1) if over_tok}
    direct = {}
    step = count // 2
    while step:
        direct[step] = exchange(own, "lat", step)
        step //= 2
    held = {0: own}
    crossed = {1: direct[1]}
    far = {k: exchange(value, "tok", 2) for k, value in ((0, own), (1, direct[1])) if over_tok}
    early = [value for k, value in direct.items() if k < count // 2]
    early += [far[k] for k in far if k == 0]
    step = count // 2
    while step > 1:
        if beside:
            early += beside.pop(0)
        fresh = {
            k | step: exchange(value, "lat", step) if k else direct[step] for k, value in held.items()
        }
        for k, value in held.items():
            if k | 1 not in crossed:
                crossed[k | 1] = exchange(value, "lat", 1)
                early.append(crossed[k | 1])
        if step < count // 2:
            if over_tok:
                early.append(far[1])
            else:
                crossed[step | 1] = exchange(direct[step], "lat", 1)
                early.append(crossed[step | 1])
        for k, value in fresh.items():
            held[k] = value if k in direct and k < count // 2 else after(value, *early)
        early = []
        step //= 2
    for k, value in held.items():
        if k | 1 not in crossed:
            crossed[k | 1] = exchange(value, "lat", 1)
    held.update(crossed)
    return [held[k] for k in range(count)], far


def stack_kernel(*refs):
    for i, ref in enumerate(refs[:-1]):
        refs[-1][i] = ref[...]


def stack(blocks):
    return pl.pallas_call(
        stack_kernel,
        out_shape=jax.ShapeDtypeStruct((len(blocks), *blocks[0].shape), blocks[0].dtype),
        compiler_params=pltpu.CompilerParams(vmem_limit_bytes=VMEM_BYTES),
        cost_estimate=SMALL,
        name="stack",
    )(*blocks)


def scatter_features(pieces):
    pieces = dict(pieces)
    step = 4
    while step < lax.axis_size("lat"):
        for k in sorted(pieces, reverse=True):
            if k & step:
                sent = pieces.pop(k).astype(BF16)
                pieces[k ^ step] = pieces[k ^ step] + exchange(sent, "lat", step).astype(F32)
        step *= 2
    return pieces[0]


def run_slices(value, mask, axis):
    count = lax.axis_size("tok")
    rows = value.shape[axis] // count
    me = lax.axis_index("tok") ^ mask
    return jnp.concatenate(
        [lax.dynamic_slice_in_dim(value, (me ^ r) * rows, rows, axis) for r in range(0, count, 2)],
        axis=axis,
    )


def weight_copies(place, w_ref, buffer, sems, half):
    latents, layers, full = w_ref.shape
    pairs, parts, height, width = buffer.shape
    block = width // 2
    runs = lax.axis_size("tok") // 2
    quarter = layers * latents // (2 * runs)
    rows = min(height, quarter)
    pieces = height // rows
    flat = w_ref.reshape(latents * layers, full)

    def copies_of(pair, part):
        copies = []
        for piece in range(pieces):
            run, row = divmod(part * height + piece * rows, quarter)
            start = (place[1] ^ (2 * run)) * quarter + row
            for b in range(2):
                column = (place[0] ^ half[2 * pair + b]) * block
                copies.append(
                    pltpu.make_async_copy(
                        flat.at[
                            pl.ds(pl.multiple_of(start, rows), rows),
                            pl.ds(pl.multiple_of(column, LANES), block),
                        ],
                        buffer.at[pair, part, pl.ds(piece * rows, rows), pl.ds(b * block, block)],
                        sems.at[((pair * parts + part) * pieces + piece) * 2 + b],
                    )
                )
        return copies

    return copies_of


def weight_buffers(weight, half, block):
    latents, layers, full = weight.shape
    runs = lax.axis_size("tok") // 2
    quarter = latents // (2 * runs)
    rows = min(LATENT_ROWS, runs * quarter)
    parts = runs * quarter // rows
    pieces = max(1, rows // quarter)
    pairs = len(half) // 2
    return (
        pltpu.VMEM((pairs, parts, layers * rows, 2 * block), BF16),
        pltpu.SemaphoreType.DMA((pairs * parts * pieces * 2,)),
    )


def encode_kernel(place, w_ref, *refs, half, mode, earlier):
    blocks = refs[:2]
    sums = refs[2:2 + earlier]
    buffer, sems, values, scratch = refs[-4:]
    rest = refs[2 + earlier:-4]
    layers = w_ref.shape[1]
    count, height, width = blocks[0].shape
    tokens = height // layers
    pairs, parts, rows, _ = buffer.shape
    step = pl.program_id(0)
    copies_of = weight_copies(place, w_ref, buffer, sems, half)

    @pl.when(step == 0)
    def _():
        for part in range(parts):
            for pair in range(pairs):
                for copy in copies_of(pair, part):
                    copy.start()
        for l in range(layers):
            for e, ref in enumerate(blocks):
                start = (2 * l + e) * tokens
                for i in range(count):
                    values[start:start + tokens, i * width:(i + 1) * width] = ref[
                        i, l * tokens:(l + 1) * tokens, :
                    ]

    for part in range(parts):

        @pl.when(step == part)
        def _():
            for pair in range(pairs):
                for copy in copies_of(pair, part):
                    copy.wait()

    product = None
    for pair in range(pairs):
        term = lax.dot_general(
            buffer[pair, step],
            values[:, pair * 2 * width:(pair + 1) * 2 * width],
            (((1,), (1,)), ((), ())),
            preferred_element_type=F32,
        )
        product = term if product is None else product + term
    sums_of = []
    for l in range(layers):
        for e in range(2):
            scratch[l, e] = product[:, (2 * l + e) * tokens:(2 * l + e + 1) * tokens]
        sums_of.append(
            jnp.concatenate(
                [scratch[l, e, pl.ds(l, rows // layers, stride=layers)] for e in range(2)], axis=1
            )
        )
    if mode == "parts":
        for l in range(layers):
            rest[0][l] = sums_of[l]
    else:
        norm_ref, bias_ref, mask_ref, across_ref, act_ref = rest
        for ref in sums:
            sums_of = [value + ref[l] for l, value in enumerate(sums_of)]
        pre = norm_ref[0] * sums_of[0] + norm_ref[1] * sums_of[1] + bias_ref[...]
        act = mask_ref[...].astype(F32).T * pre
        act_ref[...] = act.astype(BF16)
        across_ref[...] = act.T.astype(BF16)


def encode(weight, half, own, near, place, mode, sums=(), norm=None, bias=None, mask=None):
    layers, full = weight.shape[1:]
    tokens = 2 * own.shape[1] // layers
    block = own.shape[2]
    buffer, sems = weight_buffers(weight, half, block)
    _, parts, height, _ = buffer.shape
    rows = height // layers
    latents = parts * rows
    whole = pl.BlockSpec(own.shape, lambda i, s: (0, 0, 0))
    flat = pl.BlockSpec((rows, tokens), lambda i, s: (i, 0))
    split = pl.BlockSpec((layers, rows, tokens), lambda i, s: (0, i, 0))
    in_specs = [pl.BlockSpec(memory_space=pl.ANY)] + [whole] * 2
    in_specs += [flat if value.ndim == 2 else split for value in sums]
    args = [weight, own, near, *sums]
    if mode == "act":
        across = pl.BlockSpec((tokens, rows), lambda i, s: (0, i))
        in_specs += [
            pl.BlockSpec(memory_space=pltpu.SMEM),
            pl.BlockSpec((rows, 1), lambda i, s: (i, 0)),
            across,
        ]
        args += [norm, bias, mask]
        out_specs = (across, flat)
        out_shape = (
            jax.ShapeDtypeStruct((tokens, latents), BF16),
            jax.ShapeDtypeStruct((latents, tokens), BF16),
        )
    else:
        out_specs = split
        out_shape = jax.ShapeDtypeStruct((layers, latents, tokens), F32)
    return pl.pallas_call(
        functools.partial(encode_kernel, half=half, mode=mode, earlier=len(sums)),
        grid_spec=pltpu.PrefetchScalarGridSpec(
            num_scalar_prefetch=1,
            grid=(parts,),
            in_specs=in_specs,
            out_specs=out_specs,
            scratch_shapes=[
                buffer,
                sems,
                pltpu.VMEM((layers * tokens, len(half) * block), BF16),
                pltpu.VMEM((layers, 2, height, tokens // 2), F32),
            ],
        ),
        out_shape=out_shape,
        compiler_params=pltpu.CompilerParams(vmem_limit_bytes=VMEM_BYTES),
        cost_estimate=SMALL,
        name="encode_" + mode,
    )(place, *args)


def rearrange_kernel(place, *refs, halves, count):
    parts = refs[:count]
    outs = refs[-3:-1]
    wide = refs[-1]
    rows, layers, full = parts[0].shape
    chunks = full // LANES
    each = outs[0].shape[2] // len(halves[0]) // LANES
    for p, w_ref in enumerate(parts):
        for c in range(chunks):
            wide[c] = (
                w_ref[:, :, c * LANES:(c + 1) * LANES].reshape(rows * layers, LANES).astype(F32)
            )
        for half, out_ref in zip(halves, outs):
            for i, k in enumerate(half):
                for c in range(each):
                    chunk = (place[0] ^ k) * each + c
                    column = (i * each + c) * LANES
                    for l in range(layers):
                        out_ref[l, p * rows:(p + 1) * rows, column:column + LANES] = wide[
                            chunk, pl.ds(l, rows, stride=layers)
                        ].astype(BF16)


def rearrange(weight, place, halves, runs, run, earlier=()):
    latents, layers, full = weight.shape
    quarter = latents // (2 * runs)
    part = min(64, quarter // 2)
    count = 2
    rows = count * part
    steps = quarter // rows

    def index_of(p):
        return lambda i, s: (((s[1] ^ (2 * run)) * steps + i) * count + p, 0, 0)

    out = pl.BlockSpec((layers, rows, full // 2), lambda i, s: (0, run * steps + i, 0))
    shape = jax.ShapeDtypeStruct((layers, runs * quarter, full // 2), BF16)
    return pl.pallas_call(
        functools.partial(rearrange_kernel, halves=halves, count=count),
        grid_spec=pltpu.PrefetchScalarGridSpec(
            num_scalar_prefetch=1,
            grid=(steps,),
            in_specs=[pl.BlockSpec((part, layers, full), index_of(p)) for p in range(count)]
            + [pl.BlockSpec(memory_space=pl.ANY)] * len(earlier),
            out_specs=(out, out),
            scratch_shapes=[pltpu.VMEM((full // LANES, part * layers, LANES), F32)],
        ),
        out_shape=(shape, shape),
        input_output_aliases={1 + count + i: i for i in range(len(earlier))},
        compiler_params=pltpu.CompilerParams(vmem_limit_bytes=VMEM_BYTES),
        cost_estimate=SMALL,
        name="rearrange",
    )(place, *[weight] * count, *earlier)


def project_kernel(*refs, layers, mode, earlier):
    w_refs = refs[:layers]
    blocks = refs[layers:layers + 2]
    sums = refs[layers + 2:layers + 2 + earlier]
    values = refs[-1]
    rest = refs[layers + 2 + earlier:-1]
    count, height, width = blocks[0].shape
    tokens = height // layers

    @pl.when(pl.program_id(0) == 0)
    def _():
        for e, ref in enumerate(blocks):
            for l in range(layers):
                for i in range(count):
                    values[l, e * tokens:(e + 1) * tokens, i * width:(i + 1) * width] = ref[
                        i, l * tokens:(l + 1) * tokens, :
                    ]

    parts = [
        lax.dot_general(
            w_refs[l][0], values[l], (((1,), (1,)), ((), ())), preferred_element_type=F32
        )
        for l in range(layers)
    ]
    if mode == "sum":
        rest[0][...] = parts[0] + parts[1]
    else:
        total = parts[0] + parts[1]
        for ref in sums:
            total = total + ref[...]
        grad = (rest[0][...].astype(F32).T * total).astype(BF16)
        if len(rest) == 2:
            rest[1][...] = grad
        else:
            own = 2 * pl.program_id(0) < pl.num_programs(0)

            @pl.when(own)
            def _():
                rest[1][...] = grad

            @pl.when(jnp.logical_not(own))
            def _():
                rest[2][...] = grad


def project(matrix, own, near, mode, sums=(), mask=None):
    layers, latents, width = matrix.shape
    tokens = 2 * own.shape[1] // layers
    rows = min(LATENT_ROWS, latents)
    whole = pl.BlockSpec(own.shape, lambda i: (0, 0, 0))
    flat = pl.BlockSpec((rows, tokens), lambda i: (i, 0))
    across = pl.BlockSpec((tokens, rows), lambda i: (0, i))

    def layer(l):
        return pl.BlockSpec((1, rows, width), lambda i: (l, i, 0))

    in_specs = [layer(l) for l in range(layers)] + [whole] * 2
    in_specs += [flat] * len(sums)
    args = [matrix] * layers + [own, near, *sums]
    steps = latents // rows
    out_specs = flat
    out_shape = jax.ShapeDtypeStruct((latents, tokens), BF16 if mode == "grad" else F32)
    if mode == "grad":
        in_specs.append(across)
        args.append(mask)
        if steps > 1:
            middle = steps // 2
            out_specs = (
                pl.BlockSpec((rows, tokens), lambda i: (jnp.minimum(i, middle - 1), 0)),
                pl.BlockSpec((rows, tokens), lambda i: (jnp.maximum(i, middle) - middle, 0)),
            )
            out_shape = (jax.ShapeDtypeStruct((latents // 2, tokens), BF16),) * 2
    out = pl.pallas_call(
        functools.partial(project_kernel, layers=layers, mode=mode, earlier=len(sums)),
        grid=(steps,),
        in_specs=in_specs,
        out_specs=out_specs,
        scratch_shapes=[pltpu.VMEM((layers, tokens, width), BF16)],
        out_shape=out_shape,
        compiler_params=pltpu.CompilerParams(vmem_limit_bytes=VMEM_BYTES),
        cost_estimate=SMALL,
        name="project_" + mode,
    )(*args)
    if mode == "grad" and steps == 1:
        return out[:latents // 2], out[latents // 2:]
    return out


def recon_kernel(act_ref, *refs, parts):
    w_refs = refs[:parts]
    keep_ref = refs[parts]
    send_refs = refs[parts + 1:]
    depth = w_refs[0].shape[1]
    product = None
    for p, w_ref in enumerate(w_refs):
        term = jnp.dot(
            act_ref[:, p * depth:(p + 1) * depth], w_ref[0], preferred_element_type=F32
        )
        product = term if product is None else product + term
    blocks, own, width = keep_ref.shape
    for i in range(blocks):
        keep_ref[i] = product[:own, i * width:(i + 1) * width]
    if len(send_refs) == 1:
        for i in range(blocks):
            send_refs[0][i] = product[own:, i * width:(i + 1) * width].astype(BF16)
    else:
        for pair in range(len(send_refs) // 2):

            @pl.when(pl.program_id(0) == pair)
            def _():
                for i in range(2):
                    send_refs[2 * pair + i][...] = product[
                        own:, i * width:(i + 1) * width
                    ].astype(BF16)


def recon_half(act, matrix, blocks, apart):
    layers, latents, full = matrix.shape
    width = full // blocks
    tokens = act.shape[0] // 2
    parts = 2

    def part(p):
        return pl.BlockSpec((1, latents // parts, 2 * width), lambda i, j: (j, p, i))

    def single(b):
        def index(i, j):
            return jnp.where(i < b // 2, 0, jnp.where(i > b // 2, layers - 1, j)), 0

        return pl.BlockSpec((tokens, width), index)

    out = pl.BlockSpec((2, tokens, width), lambda i, j: (i, j, 0))
    shape = (blocks, layers * tokens, width)
    if apart:
        send_specs = [single(b) for b in range(blocks)]
        send_shapes = [jax.ShapeDtypeStruct(shape[1:], BF16)] * blocks
    else:
        send_specs, send_shapes = [out], [jax.ShapeDtypeStruct(shape, BF16)]
    keep, *send = pl.pallas_call(
        functools.partial(recon_kernel, parts=parts),
        grid=(blocks // 2, layers),
        in_specs=[pl.BlockSpec(act.shape, lambda i, j: (0, 0))] + [part(p) for p in range(parts)],
        out_specs=[out] + send_specs,
        out_shape=[jax.ShapeDtypeStruct(shape, F32)] + send_shapes,
        compiler_params=pltpu.CompilerParams(vmem_limit_bytes=VMEM_BYTES),
        cost_estimate=SMALL,
        name="recon_half",
    )(act, *[matrix] * parts)
    return keep, send


def grad_kernel(place, scale_ref, own_ref, far_ref, *refs, groups, where, sources, scaled):
    value_refs = refs[:sources]
    out_ref, values, left, wide, results, sems, out_sems = refs[sources:]
    pair, pairs = pl.program_id(0), pl.num_programs(0)
    pairs_held, layers, depth, width = values.shape
    tokens = depth // groups
    half = width // 2
    rows = out_ref.shape[0]
    blocks = len(where) // groups
    flat = out_ref.reshape(rows * layers, out_ref.shape[2])

    def copy_of(g, k, l):
        side = (k % 2) ^ place[1]
        source, index = where[g * blocks + k]
        if source is None:
            piece = value_refs[index[0]].at[place[2] ^ g, index[1]]
        elif index < 0:
            piece = value_refs[source]
        else:
            piece = value_refs[source].at[index]
        return pltpu.make_async_copy(
            piece.at[pl.ds(l * tokens, tokens)],
            values.at[
                k // 2, l, pl.ds(g * tokens, tokens), pl.ds(pl.multiple_of(side * half, LANES), half)
            ],
            sems.at[(g * blocks + k) * layers + l],
        )

    def copies_out(turn):
        part = rows * layers // 2
        return [
            pltpu.make_async_copy(
                results.at[lax.rem(turn, 2), pl.ds(i * part, part)],
                flat.at[
                    pl.ds(i * part, part),
                    pl.ds(pl.multiple_of((place[0] ^ turn) * width, LANES), width),
                ],
                out_sems.at[2 * lax.rem(turn, 2) + i],
            )
            for i in range(2)
        ]

    @pl.when(pair == 0)
    def _():
        for k in range(blocks):
            for g in range(groups):
                for l in range(layers):
                    copy_of(g, k, l).start()
        near = own_ref.shape[1]
        left[:, :near] = own_ref[...]
        left[:, near:] = far_ref[...]

    for j in range(blocks // 2):

        @pl.when(pair == j)
        def _():
            for b in range(2):
                for g in range(groups):
                    for l in range(layers):
                        copy_of(g, 2 * j + b, l).wait()

    for l in range(layers):
        product = jnp.dot(left[...], values[pair, l], preferred_element_type=F32)
        if scaled:
            product = product * scale_ref[l]
        for c in range(width // LANES):
            wide[c, pl.ds(l, rows, stride=layers)] = product[:, c * LANES:(c + 1) * LANES]

    @pl.when(pair >= 2)
    def _():
        for copy in copies_out(pair - 2):
            copy.wait()

    for c in range(width // LANES):
        results[lax.rem(pair, 2), :, c * LANES:(c + 1) * LANES] = wide[c].astype(BF16)
    for copy in copies_out(pair):
        copy.start()

    @pl.when(pair == pairs - 1)
    def _():
        for copy in copies_out(pair - 1) + copies_out(pair):
            copy.wait()


def weight_grad(own, far, sources, where, place, scale, scaled, shape):
    rows = far.shape[0]
    layers, full = shape
    groups = lax.axis_size("tok")
    depth = own.shape[1] + far.shape[1]
    blocks = len(where) // groups
    width = full // (blocks // 2)
    anywhere = pl.BlockSpec(memory_space=pl.ANY)
    return pl.pallas_call(
        functools.partial(
            grad_kernel, groups=groups, where=where, sources=len(sources), scaled=scaled
        ),
        grid_spec=pltpu.PrefetchScalarGridSpec(
            num_scalar_prefetch=1,
            grid=(blocks // 2,),
            in_specs=[
                pl.BlockSpec(memory_space=pltpu.SMEM),
                pl.BlockSpec(far.shape, lambda i, s: (0, 0)),
                pl.BlockSpec(far.shape, lambda i, s: (0, 0)),
            ]
            + [anywhere] * len(sources),
            out_specs=anywhere,
            scratch_shapes=[
                pltpu.VMEM((blocks // 2, layers, depth, width), BF16),
                pltpu.VMEM((rows, depth), BF16),
                pltpu.VMEM((width // LANES, rows * layers, LANES), F32),
                pltpu.VMEM((2, rows * layers, width), BF16),
                pltpu.SemaphoreType.DMA((groups * blocks * layers,)),
                pltpu.SemaphoreType.DMA((4,)),
            ],
        ),
        out_shape=jax.ShapeDtypeStruct((rows, layers, full), BF16),
        compiler_params=pltpu.CompilerParams(vmem_limit_bytes=VMEM_BYTES),
        cost_estimate=pl.CostEstimate(
            flops=4 * rows * depth * layers * full,
            bytes_accessed=8 * rows * layers * full,
            transcendentals=0,
        ),
        name="weight_grad",
    )(place, scale, own, far, *sources)


def per_device(streams, active_mask, enc_weight, enc_bias, dec_weight, dec_bias):
    lat_count = lax.axis_size("lat")
    tok_count = lax.axis_size("tok")
    tok_dev, layers, width_part = streams.shape
    full_width = width_part * lat_count
    tokens = tok_dev * tok_count
    me = lax.axis_index("lat")
    aligned = width_part % LANES == 0
    block_count = lat_count if aligned else 8
    block_width = full_width // block_count
    here = me if aligned else jnp.zeros_like(me)

    own_x = streams.transpose(1, 0, 2).reshape(layers * tok_dev, width_part)
    own_f = own_x.astype(F32).reshape(layers, tok_dev, width_part)
    runs = tok_count // 2
    tok_me = lax.axis_index("tok")
    halves = block_order(block_count)
    spot = jnp.stack([here, tok_me]).astype(jnp.int32)
    place = jnp.stack([here >> 1, here & 1, tok_me]).astype(jnp.int32)

    mask_low = active_mask.astype(BF16)
    mask_far = exchange(run_slices(mask_low, 1, 1), "tok", 1)
    mask = jnp.concatenate([run_slices(mask_low, 0, 1), mask_far], axis=0)
    bias = run_slices(enc_bias.reshape(-1, 1), 0, 0)

    def gather_halves(own, multiply, beside=(), over_tok=False):
        blocks, far = gather_features(own, beside, over_tok)
        first = stack([blocks[k] for k in halves[0]])
        first_near = exchange(first, "tok", 1)
        sums = multiply(first, first_near)
        squared = squares(first, layers)
        early = [sums, squared]
        if over_tok:
            far.update({k: exchange(blocks[k], "tok", 2) for k in (4, 2)})
            early += [far[4], far[2]]
        final = halves[1][-1]
        blocks[final] = after(blocks[final], *early)
        second = stack([blocks[k] for k in halves[1]])
        near = [first_near, exchange(second, "tok", 1)]
        return blocks, [first, second], near, sums, squared, far

    dec_first = rearrange(dec_weight, spot, halves, runs, 0)
    dec_halves = rearrange(dec_weight, spot, halves, runs, 1, dec_first)
    _, x_own, x_near, sums, squared, _ = gather_halves(
        own_x,
        lambda own, near: encode(enc_weight, halves[0], own, near, spot, "parts"),
        beside=([*dec_first, mask, bias], dec_halves),
    )
    square_sums = jnp.sum(sum_tokens(squared + squares(x_own[1], layers)), axis=(1, 2))
    norm_scale = lax.rsqrt(square_sums / (tokens * full_width) + 1e-06)
    act_across, act = encode(
        enc_weight, halves[1], x_own[1], x_near[1], spot, "act", [sums], norm_scale, bias, mask
    )
    x_all = [lax.all_gather(value, "tok") for value in x_own]
    quarter = act.shape[0] // runs

    bias_part = lax.dynamic_slice_in_dim(dec_bias, me * width_part, width_part, 1)
    keep, send = recon_half(act_across, dec_halves[1], block_count // 2, False)
    send = exchange(send[0], "tok", 1)
    starts = range(block_count // 2 - 2, -2, -2)
    if aligned:
        bundles = [
            (keep[start:start + 2] + send[start:start + 2].astype(F32)).astype(BF16)
            for start in starts
        ]
        act_across = after(act_across, *bundles)
        bundles = [exchange(bundle, "lat", 1) for bundle in bundles]
    else:
        cross = keep + send.astype(F32)
    keep, send = recon_half(act_across, dec_halves[0], block_count // 2, True)
    send = [exchange(value, "tok", 1) for value in send]
    act_far = exchange(act[quarter:], "tok", 2)
    if aligned:
        pieces = {}
        received = None
        for start, bundle in zip(starts, bundles):
            if received is not None:
                bundle = after(bundle, received)
            low, high = [
                keep[i] + send[i].astype(F32) + bundle[i - start].astype(F32)
                for i in (start, start + 1)
            ]
            received = exchange(high.astype(BF16), "lat", 2)
            pieces[2 * start] = low + received.astype(F32)
        recon = scatter_features(pieces)
    else:
        own = keep + jnp.stack(send).astype(F32)
        whole = jnp.stack([own, cross], axis=1).reshape(block_count, layers * tok_dev, block_width)
        whole = whole.transpose(1, 0, 2).reshape(layers * tok_dev, full_width)
        recon = lax.psum_scatter(whole, "lat", scatter_dimension=1, tiled=True)
    recon = after(recon, act_far, *x_all)

    recon = recon.reshape(layers, tok_dev, width_part) + bias_part[:, None]
    diff = recon - norm_scale[:, None, None] * own_f
    factor = LOSS_SCALE / tokens
    err_low = (diff * factor).astype(BF16).reshape(layers * tok_dev, width_part)
    err_blocks, err_own, err_near, sums, squared, far = gather_halves(
        err_low, lambda own, near: project(dec_halves[0], own, near, "sum"), over_tok=True
    )
    far.update({k: exchange(err_blocks[k], "tok", 2) for k in (6, 5)})
    grad, grad_away = project(dec_halves[1], err_own[1], err_near[1], "grad", [sums], mask=mask)
    grad_far = exchange(grad_away, "tok", 2)
    for k, value in ((3, far[2]), (7, after(far[6], grad_away))):
        far[k] = exchange(value, "lat", 1) if aligned else exchange(err_blocks[k], "tok", 2)
    error_sums = squared + squares(err_own[1], layers)
    late = (3, 5, 6, 7)
    grad_far, error_sums, *values = lax.optimization_barrier(
        (grad_far, error_sums, *[far[k] for k in late])
    )
    far.update(zip(late, values))
    last = {k: exchange(value, "tok", 1) for k, value in far.items()}

    shape = (layers, full_width)
    spots = {k: (h, i) for h, half in enumerate(halves) for i, k in enumerate(half)}
    order = [spots[k] for k in range(block_count)]
    enc_grad = weight_grad(
        grad, grad_far, x_all, [(None, spot) for spot in order] * tok_count, place,
        norm_scale, True, shape,
    )
    error_sums = sum_tokens(error_sums)
    act, error_sums = lax.optimization_barrier((act, error_sums))
    where = [(2 * g + h, i) for g in range(2) for h, i in order]
    where += [(4 + g * block_count + k, -1) for g in range(2) for k in range(block_count)]
    sources = err_own + err_near + [group[k] for group in (far, last) for k in range(block_count)]
    dec_grad = weight_grad(act, act_far, sources, where, place, norm_scale, False, shape)
    mean_error = jnp.sum(error_sums) / (factor * factor * tokens * layers * full_width)
    return (enc_grad, dec_grad, mean_error)


def solution(mesh):
    in_specs = (
        P("tok", None, "lat"),
        P("tok", "lat"),
        P("lat", None, None),
        P("lat"),
        P("lat", None, None),
        P(),
    )
    out_specs = (P(("lat", "tok"), None, None), P(("lat", "tok"), None, None), P())
    return jax.shard_map(
        per_device, mesh=mesh, in_specs=in_specs, out_specs=out_specs, check_vma=False
    )
```
